128 devices in a mesh: aperture: 16 (over x_hi, z, core), range: 8 (over y, x_lo).
Axes of the slice: x: 4 (x_hi: 2, x_lo: 2; x = x_hi * 2 + x_lo), y: 4, z: 4, core: 2. Of those that a mesh axis runs over, the one named last changes fastest.
Arguments:
- child_image: float32 [2, 4096, 8192], P(None, 'aperture', 'range'), may hold values from -6 to 6
- tap_weights: float32 [4, 2, 4, 4096], P(None, None, None, 'aperture'), may hold values from -3 to 3
- band_offsets: int32 [4, 2, 4096], P(None, None, 'aperture'), may hold values from 0 to 252, as said below
- range_shift: float32 [4, 2, 4096], P(None, None, 'aperture'), may hold values from -1 to 1
- phase_base: float32 [4, 2, 4096], P(None, None, 'aperture'), may hold values from -3.140625 to 3.140625
- phase_slope: float32 [4, 2, 4096], P(None, None, 'aperture'), may hold values from -6 to 6
- tile_sources: int32 [16, 8], P('aperture'), may hold values from 0 to 15, as said below
- tile_counts: int32 [16], P('aperture'), may hold values from 1 to 8
- resample_weights: bfloat16 [16, 8, 512, 256], P('aperture'), may hold values from -0.1875 to 0.1875
Outputs:
- ground_image: float32 [2, 8192, 8192], P(None, 'aperture', 'range')
The draws below stay inside these ranges and needn't reach their ends.
Inputs may be any that keep to these rules, and one draw needn't show every extreme that they name: band_offsets[l, s, a * 256 + q] lies between h * 128 and h * 128 + 256 / 2 - 4, where h is bit l of a; both ends are reached. `tile_sources`: the first tile_counts[g] entries of row g are different beam blocks; entries past the count are ignored; some tile lists 8 blocks.
All inputs are finite; a program needn't handle non-finite values.
Results may differ from the reference program's by a relative error of at most 0.0029.
Values may be sent and summed in bfloat16 or wider, within the bound.
A program may use at most 128 MiB of HBM per device.

```python
import jax
import jax.numpy as jnp
from jax import lax

RANGE = 8192
BEAMS = 256
TAPS = 4
K_MAX = 8
LEVELS = 4
APERTURE_BEAMS = 4096
COLS = 512
N_APERTURE = 16


def tile_lists(key):
    blocks_total = APERTURE_BEAMS // BEAMS
    starts = jax.random.randint(jax.random.fold_in(key, 101), (blocks_total,), 0, blocks_total, dtype=jnp.int32)
    counts = jax.random.randint(jax.random.fold_in(key, 102), (blocks_total,), 1, K_MAX + 1, dtype=jnp.int32)
    picked_tile = jax.random.randint(jax.random.fold_in(key, 103), (), 0, blocks_total, dtype=jnp.int32)
    counts = jnp.where(jnp.arange(blocks_total, dtype=jnp.int32) == picked_tile, K_MAX, counts).astype(jnp.int32)
    slot_ids = jnp.arange(K_MAX, dtype=jnp.int32)
    sources = ((starts[:, None] + slot_ids[None, :]) % blocks_total).astype(jnp.int32)
    return (sources, counts)


def draw_band_offsets(key, part):
    subkey = jax.random.fold_in(key, 11)
    row_ids = jnp.arange(APERTURE_BEAMS, dtype=jnp.int32)
    device_ids = row_ids // BEAMS
    beam_ids = row_ids % BEAMS
    level_ids = jnp.arange(LEVELS, dtype=jnp.int32)[:, None, None]
    half_bit = jnp.bitwise_and(jnp.right_shift(device_ids[None, None, :], level_ids), 1)
    jitter = jax.random.randint(subkey, (LEVELS, 2, APERTURE_BEAMS), 0, 3, dtype=jnp.int32)
    inside = jnp.clip(beam_ids[None, None, :] // 2 - 2 + jitter, 0, BEAMS // 2 - TAPS)
    return (inside + half_bit * (BEAMS // 2)).astype(jnp.int32)


def draw_tile_sources(key, part):
    sources, counts = tile_lists(key)
    return sources


def draw_tile_counts(key, part):
    sources, counts = tile_lists(key)
    return counts


def block_levels(stream_key, dims, cuts, smallest, largest):
    level, own = 1.0, jax.random.fold_in(stream_key, 6)
    for dim, shards_of in cuts:
        steps = jnp.exp(jax.random.uniform(jax.random.fold_in(own, dim), (shards_of,), jnp.float32, smallest / len(cuts), largest / len(cuts)))
        level = level * jnp.repeat(steps, dims[dim] // shards_of).reshape([-1 if axis == dim else 1 for axis in range(len(dims))])
    return level


def gaussian(rng, dims, width, most, shards=(), kind=jnp.bfloat16):
    values = width * jax.random.normal(rng, dims, jnp.float32)
    if shards:
        values = values * block_levels(rng, dims, shards, -0.22, 0.18)
    return jnp.clip(values, -most, most).astype(kind)


def setup_inputs(seed: int = 0) -> dict:
    key_list = jax.random.split(jax.random.key(seed), 10)
    child_image = gaussian(key_list[0], (2, APERTURE_BEAMS, RANGE), 1.0, 6.0, ((1, 16), (2, 8)), jnp.float32)
    tap_weights = gaussian(key_list[1], (LEVELS, 2, TAPS, APERTURE_BEAMS), 0.5, 3.0, ((3, 16),), jnp.float32)
    band_offsets = draw_band_offsets(jax.random.fold_in(key_list[9], 71), 0)
    range_shift = jnp.clip(jax.random.uniform(key_list[3], (LEVELS, 2, APERTURE_BEAMS), jnp.float32, -1.0, 1.0) * block_levels(key_list[3], (LEVELS, 2, APERTURE_BEAMS), ((2, 16),), -0.4, 0.0), -1.0, 1.0)
    phase_base = jnp.clip(jax.random.uniform(key_list[4], (LEVELS, 2, APERTURE_BEAMS), jnp.float32, -3.140625, 3.140625), -3.140625, 3.140625)
    phase_slope = jnp.clip(jax.random.uniform(key_list[5], (LEVELS, 2, APERTURE_BEAMS), jnp.float32, -6.0, 6.0) * block_levels(key_list[5], (LEVELS, 2, APERTURE_BEAMS), ((2, 16),), -0.4, 0.0), -6.0, 6.0)
    tile_sources = draw_tile_sources(jax.random.fold_in(key_list[9], 71), 0)
    tile_counts = draw_tile_counts(jax.random.fold_in(key_list[9], 71), 0)
    resample_weights = gaussian(key_list[8], (N_APERTURE, K_MAX, COLS, BEAMS), (4 * BEAMS) ** -0.5, 0.1875, ((0, 16),))
    return {"child_image": child_image, "tap_weights": tap_weights, "band_offsets": band_offsets, "range_shift": range_shift, "phase_base": phase_base, "phase_slope": phase_slope, "tile_sources": tile_sources, "tile_counts": tile_counts, "resample_weights": resample_weights}


merge_scale = 0.70710678


def finish_side(beam_part, shifts, base_phase, slope_phase, radius):
    center = beam_part[:, :, 1:-1]
    range_next = beam_part[:, :, 2:]
    range_prev = beam_part[:, :, :-2]
    shifts = shifts[:, None]
    shifted = center + jnp.maximum(shifts, 0.0) * (range_next - center) + jnp.maximum(-shifts, 0.0) * (range_prev - center)
    angles = base_phase[:, None] + slope_phase[:, None] * radius[None, :]
    cosine = jnp.cos(angles)
    sine_part = jnp.sin(angles)
    real_part = shifted[0] * cosine - shifted[1] * sine_part
    imag_part = shifted[0] * sine_part + shifted[1] * cosine
    return jnp.stack([real_part, imag_part])


def reference(child_image, tap_weights, band_offsets, range_shift, phase_base, phase_slope, tile_sources, tile_counts, resample_weights):
    radius = jnp.arange(RANGE, dtype=jnp.float32) / RANGE
    tap_index = jnp.arange(TAPS, dtype=jnp.int32)
    current = child_image
    for merge_level in range(LEVELS):
        blocks = current.reshape(2, N_APERTURE, BEAMS, RANGE)
        padded = jnp.pad(blocks, ((0, 0), (0, 0), (0, 0), (1, 1)))
        level_mask = 1 << merge_level

        def merge_one(device):
            lower_index = jnp.bitwise_and(device, ~level_mask).astype(jnp.int32)
            upper_index = jnp.bitwise_or(device, level_mask).astype(jnp.int32)
            start_row = (device * BEAMS).astype(jnp.int32)
            parent = jnp.zeros((2, BEAMS, RANGE), jnp.float32)
            for child_side, child_index in ((0, lower_index), (1, upper_index)):
                child_rows = lax.dynamic_index_in_dim(padded, child_index, 1, keepdims=False)
                weights = lax.dynamic_slice_in_dim(tap_weights[merge_level, child_side], start_row, BEAMS, 1)
                offsets = lax.dynamic_slice_in_dim(band_offsets[merge_level, child_side], start_row, BEAMS, 0).astype(jnp.int32)
                shifts = lax.dynamic_slice_in_dim(range_shift[merge_level, child_side], start_row, BEAMS, 0)
                base_phase = lax.dynamic_slice_in_dim(phase_base[merge_level, child_side], start_row, BEAMS, 0)
                slope_phase = lax.dynamic_slice_in_dim(phase_slope[merge_level, child_side], start_row, BEAMS, 0)
                row_index = offsets[None, :] + tap_index[:, None]
                picked = child_rows[:, row_index, :]
                beam_part = jnp.sum(picked * weights[None, :, :, None], axis=1)
                parent = parent + finish_side(beam_part, shifts, base_phase, slope_phase, radius)
            return parent * merge_scale

        parents = lax.map(merge_one, jnp.arange(N_APERTURE, dtype=jnp.int32))
        current = jnp.transpose(parents, (1, 0, 2, 3)).reshape(2, N_APERTURE * BEAMS, RANGE)
    polar_image = current.astype(jnp.bfloat16).reshape(2, N_APERTURE, BEAMS, RANGE)

    def ground_tile(tile_index):
        def add_slot(slot_index, running):
            source = tile_sources[tile_index, slot_index].astype(jnp.int32)
            block_image = lax.dynamic_index_in_dim(polar_image, source, 1, keepdims=False)
            matrix = resample_weights[tile_index, slot_index]

            def product():
                real_part = jnp.dot(matrix, block_image[0], preferred_element_type=jnp.float32)
                imag_part = jnp.dot(matrix, block_image[1], preferred_element_type=jnp.float32)
                return running + jnp.stack([real_part, imag_part])

            def unchanged():
                return running

            return lax.cond(slot_index < tile_counts[tile_index], product, unchanged)

        return lax.fori_loop(0, K_MAX, add_slot, jnp.zeros((2, COLS, RANGE), jnp.float32))

    tiles = lax.map(ground_tile, jnp.arange(N_APERTURE, dtype=jnp.int32))
    return jnp.transpose(tiles, (1, 0, 2, 3)).reshape(2, N_APERTURE * COLS, RANGE)
```

```python
import functools

import jax
import jax.numpy as jnp
from jax import lax
from jax.experimental import pallas as pl
from jax.experimental.pallas import tpu as pltpu
from jax.sharding import PartitionSpec as P

RANGE = 8192
SCALE = 0.70710678
MESH = pl.DeviceIdType.MESH
SUBS = 2
ROWS = 64
TILES = 9
F32 = jnp.float32
BF16 = jnp.bfloat16


def kernel(
    child, taps, bands, shifts, bases, slopes, sources_v, counts_v, matrices, sources, counts,
    out,
    staged, edges, received, split, part, bank, wave, rates, own_par, par,
    g00, g01, g10, g11, g20, g21, g30, g31,
    other_mat, wide, columns, sent_tiles, got_tiles, held, info, info_got, info_s,
    a2a_send, a2a_recv, edge_send, edge_recv, par_send, par_recv, pary_send, pary_recv,
    mat_send, mat_recv, maty_send, maty_recv, ring_send, ring_recv, relay_send, relay_recv,
    core_send, core_recv, tile_send, tile_recv, info_send, info_recv, local_sem,
):
    gathered = ((g00, g01), (g10, g11), (g20, g21), (g30, g31))
    a = lax.axis_index("aperture")
    p = lax.axis_index("range")
    core, z, xh = a % 2, (a // 2) % 4, a // 8
    y, xl = p // 2, p % 2
    me = a // 2
    sibling = (me * 2 + 1 - core, p)
    z_next = (xh * 8 + ((z + 1) % 4) * 2 + core, p)
    z_prev = (xh * 8 + ((z + 3) % 4) * 2 + core, p)
    x_pair = ((a + 8) % 16, p)
    x_side = ((a + 8) % 16, y * 2 + 1 - xl)
    r_next = (a, (p + 1) % 8)
    r_prev = (a, (p + 7) % 8)

    def y_peer(step):
        return (a, ((y + step) % 4) * 2 + xl)

    barrier = pltpu.get_barrier_semaphore()

    def greet(step, carry):
        pl.semaphore_signal(barrier, inc=1, device_id=((a + step) % 16, p), device_id_type=MESH)
        return carry

    lax.fori_loop(1, 16, greet, 0)
    for peer in (x_side, r_next, r_prev, y_peer(1), y_peer(2), y_peer(3)):
        pl.semaphore_signal(barrier, inc=1, device_id=peer, device_id_type=MESH)

    for level in range(4):
        for side in range(2):
            row = side * 8
            own_par[level, row : row + 4, :] = taps[level, side]
            own_par[level, row + 4 : row + 5, :] = bands[level, side : side + 1, :].astype(F32)
            own_par[level, row + 5 : row + 6, :] = shifts[level, side : side + 1, :]
            own_par[level, row + 6 : row + 7, :] = bases[level, side : side + 1, :]
            own_par[level, row + 7 : row + 8, :] = slopes[level, side : side + 1, :]
    info[...] = jnp.zeros((8, 128), jnp.int32)
    info[0:1, 0:8] = sources_v[...]
    info[1:2, 0:1] = counts_v[...]

    pl.semaphore_wait(barrier, 21)

    def remote(src, dst, send, recv, to):
        return pltpu.make_async_remote_copy(
            src_ref=src, dst_ref=dst, send_sem=send, recv_sem=recv, device_id=to, device_id_type=MESH
        )

    def par_copy(step, slot):
        return remote(
            own_par.at[y], par.at[y, slot], par_send.at[step], par_recv.at[slot], ((a + 2 * step) % 16, p)
        )

    def send_par(step, carry):
        par_copy(step, me).start()
        return carry

    lax.fori_loop(1, 8, send_par, 0)
    mat_copy = remote(
        matrices.at[pl.ds(2 * y, 2)], other_mat.at[pl.ds(2 * y, 2)], mat_send.at[0], mat_recv.at[0], x_side
    )
    mat_copy.start()
    info_copy = remote(info, info_got, info_send.at[0], info_recv.at[0], x_pair)
    info_copy.start()

    def turn(k, carry):
        for comp in range(2):
            for half in range(2):
                block = child[comp, half * 128 : half * 128 + 128, pl.ds(pl.multiple_of(k * 128, 128), 128)]
                block = block.T.reshape(2, 8, 8, 128)
                for sub in range(2):
                    staged[k * 2 + sub, half, 0:8, comp] = block[sub]
        return carry

    lax.fori_loop(0, 8, turn, 0)
    edge_next = remote(staged.at[15, :, 7], edges.at[0], edge_send.at[0], edge_recv.at[0], r_next)
    edge_prev = remote(staged.at[0, :, 0], edges.at[1], edge_send.at[1], edge_recv.at[1], r_prev)
    edge_next.start()
    edge_prev.start()
    low = lax.broadcasted_iota(jnp.int32, (8, 128), 0) < 4

    def fill(j, carry):
        for half in range(2):
            for comp in range(2):
                staged[j, half, 8, comp] = jnp.where(low, staged[j + 1, half, 0, comp], staged[j - 1, half, 7, comp])
        return carry

    lax.fori_loop(1, 15, fill, 0)
    edge_next.wait()
    edge_prev.wait()
    has_prev = jnp.where(p > 0, 1.0, 0.0).astype(F32)
    has_next = jnp.where(p < 7, 1.0, 0.0).astype(F32)
    for half in range(2):
        for comp in range(2):
            staged[0, half, 8, comp] = jnp.where(low, staged[1, half, 0, comp], edges[0, half, comp] * has_prev)
            staged[15, half, 8, comp] = jnp.where(low, edges[1, half, comp] * has_next, staged[14, half, 7, comp])

    def child_copy(sub, step, slot):
        to = (a + step) % 16
        return remote(
            staged.at[(to // 2) * 2 + sub, to % 2],
            received.at[sub, slot],
            a2a_send.at[sub, step],
            a2a_recv.at[sub, slot],
            (to, p),
        )

    for sub in range(SUBS):

        def send_child(step, carry, sub=sub):
            child_copy(sub, step, a).start()
            return carry

        lax.fori_loop(1, 16, send_child, 0)
        pltpu.make_async_copy(staged.at[me * 2 + sub, core], received.at[sub, a], local_sem.at[sub]).start()

    par[y, me] = own_par[y]

    def wait_par(step, carry):
        par_copy(step, (me + step) % 8).wait_recv()
        return carry

    lax.fori_loop(1, 8, wait_par, 0)

    def pary_copy(step):
        return remote(par.at[y], par.at[y], pary_send.at[step], pary_recv.at[step], y_peer(step))

    def pary_wait(step):
        there = (y + 4 - step) % 4
        remote(par.at[there], par.at[there], pary_send.at[step], pary_recv.at[step], y_peer(step)).wait_recv()

    for step in (1, 2, 3):
        pary_copy(step).start()
    for step in (1, 2, 3):
        pary_wait(step)

    first = p * 1024 + me * (SUBS * ROWS)
    beam = lax.broadcasted_iota(jnp.int32, (128, 256), 0).astype(F32)
    radius = (first + lax.broadcasted_iota(jnp.int32, (8, 256), 0)).astype(F32) * (1.0 / RANGE)
    for level in range(4):

        def prepare(q, carry, level=level):
            half = core if level == 0 else (q // (1 << (level - 1))) % 2
            start = (half * 128).astype(F32)
            for side in range(2):
                index = (level * 8 + q) * 2 + side
                rows = par[level, q, side * 8 : side * 8 + 8, :]
                offset = beam - (rows[4:5] - start)
                banded = jnp.zeros((128, 256), F32)
                for tap in range(4):
                    banded = jnp.where(offset == float(tap), rows[tap : tap + 1], banded)
                high = banded.astype(BF16)
                bank[index, 0:128] = high
                bank[index, 128:256] = (banded - high.astype(F32)).astype(BF16)
                angle = rows[6:7] + rows[7:8] * radius
                wave[index, 0] = SCALE * jnp.cos(angle)
                wave[index, 1] = SCALE * jnp.sin(angle)
                step = rows[7:8] * (8.0 / RANGE)
                rates[index, 0:1] = jnp.cos(step)
                rates[index, 1:2] = jnp.sin(step)
                rates[index, 2:3] = jnp.abs(rows[5:6])
                rates[index, 3:4] = rows[5:6]
            return carry

        lax.fori_loop(0, 8, prepare, 0)

    live = counts[0, 0]
    for k in range(8):
        wide[0, :, k * 256 : k * 256 + 256] = matrices[k] * jnp.where(k < live, 1.0, 0.0).astype(BF16)

    mat_copy.wait_recv()

    def maty_copy(step):
        own = pl.ds(2 * y, 2)
        return remote(other_mat.at[own], other_mat.at[own], maty_send.at[step], maty_recv.at[step], y_peer(step))

    def maty_wait(step):
        there = pl.ds(2 * ((y + 4 - step) % 4), 2)
        remote(other_mat.at[there], other_mat.at[there], maty_send.at[step], maty_recv.at[step], y_peer(step)).wait_recv()

    for step in (1, 2, 3):
        maty_copy(step).start()

    row8 = lax.broadcasted_iota(jnp.int32, (8, 128), 0)

    def run_level(level, sub):
        source, target = split.at[level % 2], split.at[(level + 1) % 2]
        start = first + sub * ROWS
        bins = start + jnp.where(low, ROWS + row8, row8 - 8)
        inside = jnp.where((bins >= 0) & (bins < RANGE), 1.0, 0.0).astype(F32)

        def one(q, carry):
            index = (level * 8 + q) * 2
            for side in range(2):
                if level == 0:
                    slot = 2 * q + side
                else:
                    bit = 1 << (level - 1)
                    half = (q // bit) % 2
                    slot = (q - half * bit + side * bit) * 2 + half
                x = source[slot]
                w = bank[index + side]
                high, rest = w[0:128], w[128:256]
                part[side] = jnp.dot(
                    jnp.concatenate([x, x], axis=1),
                    jnp.concatenate([high, high, rest, rest], axis=0),
                    preferred_element_type=F32,
                )
            for half in range(2):
                lanes = slice(half * 128, half * 128 + 128)

                def load(side, comp, t):
                    return part[side, t * 16 + comp * 8 : t * 16 + comp * 8 + 8, lanes]

                cosine = [wave[index + s, 0, :, lanes] for s in range(2)]
                sine = [wave[index + s, 1, :, lanes] for s in range(2)]
                step_c = [jnp.broadcast_to(rates[index + s, 0:1, lanes], (8, 128)) for s in range(2)]
                step_s = [jnp.broadcast_to(rates[index + s, 1:2, lanes], (8, 128)) for s in range(2)]
                amount = [jnp.broadcast_to(rates[index + s, 2:3, lanes], (8, 128)) for s in range(2)]
                ahead = [jnp.broadcast_to(rates[index + s, 3:4, lanes], (8, 128)) > 0.0 for s in range(2)]
                back_c = [cosine[s] * step_c[s] + sine[s] * step_s[s] for s in range(2)]
                back_s = [sine[s] * step_c[s] - cosine[s] * step_s[s] for s in range(2)]
                up, down = {}, {}
                for s in range(2):
                    for comp in range(2):
                        up[s, comp, 0] = pltpu.roll(load(s, comp, 0), 7, 0)
                        down[s, comp, -1] = pltpu.roll(load(s, comp, TILES - 1), 1, 0)
                previous = None
                for t in range(TILES if level < 3 else TILES - 1):
                    if t == TILES - 1:
                        if sub + 1 < SUBS:
                            for s in range(2):
                                wave[index + s, 0, :, lanes] = cosine[s]
                                wave[index + s, 1, :, lanes] = sine[s]
                        for s in range(2):
                            cosine[s] = jnp.where(low, cosine[s], back_c[s])
                            sine[s] = jnp.where(low, sine[s], back_s[s])
                    total = [None, None]
                    for s in range(2):
                        moved = []
                        for comp in range(2):
                            center = load(s, comp, t)
                            if t + 1 < TILES:
                                up[s, comp, t + 1] = pltpu.roll(load(s, comp, t + 1), 7, 0)
                                following = up[s, comp, t + 1]
                            else:
                                following = pltpu.roll(load(s, comp, 0), 7, 0)
                            down[s, comp, t] = pltpu.roll(center, 1, 0)
                            after = jnp.where(row8 == 7, following, up[s, comp, t])
                            before = jnp.where(row8 == 0, down[s, comp, t - 1], down[s, comp, t])
                            beside = jnp.where(ahead[s], after, before)
                            moved.append(center + amount[s] * (beside - center))
                        real = moved[0] * cosine[s] - moved[1] * sine[s]
                        imag = moved[0] * sine[s] + moved[1] * cosine[s]
                        total = [real, imag] if s == 0 else [total[0] + real, total[1] + imag]
                        if t < TILES - 1:
                            cosine[s], sine[s] = (
                                cosine[s] * step_c[s] - sine[s] * step_s[s],
                                sine[s] * step_c[s] + cosine[s] * step_s[s],
                            )
                    if level < 3:
                        if t == TILES - 1:
                            total = [v * inside for v in total]
                        both = jnp.concatenate(total, axis=0)
                        high = both.astype(BF16)
                        target[q * 2 + half, t * 16 : t * 16 + 16, 0:128] = high
                        target[q * 2 + half, t * 16 : t * 16 + 16, 128:256] = (both - high.astype(F32)).astype(BF16)
                    elif t % 2 == 0:
                        previous = total
                    else:
                        for comp in range(2):
                            row = comp * ROWS + (t // 2) * 16
                            gathered[0][sub][core * 8 + q, row : row + 16, lanes] = jnp.concatenate(
                                [previous[comp], total[comp]], axis=0
                            ).astype(BF16)
                if level == 3 and sub + 1 < SUBS:
                    for s in range(2):
                        wave[index + s, 0, :, lanes] = cosine[s]
                        wave[index + s, 1, :, lanes] = sine[s]
            return carry

        lax.fori_loop(0, 8, one, 0)

    own_half = pl.ds(core * 8, 8)
    pending = []

    def start(copy):
        copy.start()
        pending.append(copy)

    def core_copy(place, sub):
        ref = gathered[place][sub].at[own_half]
        n = place * 2 + sub
        return remote(ref, ref, core_send.at[n], core_recv.at[n], sibling)

    def core_wait(place, sub):
        ref = gathered[place][sub].at[pl.ds((1 - core) * 8, 8)]
        n = place * 2 + sub
        remote(ref, ref, core_send.at[n], core_recv.at[n], sibling).wait_recv()

    def ring_copy(way, sub):
        n = way * 2 + sub
        return remote(
            gathered[0][sub].at[own_half], gathered[1 + way][sub].at[own_half],
            ring_send.at[n], ring_recv.at[n], (z_next, z_prev)[way],
        )

    def relay_copy(way, sub):
        n = way * 2 + sub
        quarter = pl.ds(core * 8 + way * 4, 4)
        return remote(
            gathered[1 + way][sub].at[quarter], gathered[3][sub].at[quarter],
            relay_send.at[n], relay_recv.at[n], (z_next, z_prev)[way],
        )

    for sub in range(SUBS):

        def wait_child(step, carry, sub=sub):
            child_copy(sub, step, (a + step) % 16).wait_recv()
            return carry

        lax.fori_loop(1, 16, wait_child, 0)
        pltpu.make_async_copy(staged.at[me * 2 + sub, core], received.at[sub, a], local_sem.at[sub]).wait()

        def halve(n, carry, sub=sub):
            x = received[sub, n].reshape(TILES * 16, 128)
            high = x.astype(BF16)
            split[0, n, :, 0:128] = high
            split[0, n, :, 128:256] = (x - high.astype(F32)).astype(BF16)
            return carry

        lax.fori_loop(0, 16, halve, 0)
        for level in range(4):
            run_level(level, sub)
        for way in range(2):
            start(ring_copy(way, sub))
        start(core_copy(0, sub))

    def relay(sub):
        for way in range(2):
            ring_copy(way, sub).wait_recv()
            start(relay_copy(way, sub))
            start(core_copy(1 + way, sub))

    def far(sub):
        for way in range(2):
            relay_copy(way, sub).wait_recv()
        start(core_copy(3, sub))

    def tile_copy(n):
        return remote(sent_tiles.at[n], got_tiles.at[n], tile_send.at[n], tile_recv.at[n], x_pair)

    lane = lax.broadcasted_iota(jnp.int32, (512, 128), 1)

    def place_tile(early, late, side, place):
        where = (side * 4 + (z + (0, 3, 1, 2)[place]) % 4) * 128
        lanes = pl.ds(pl.multiple_of(where, 128), 128)
        out[0, :, lanes] = jnp.where(lane < 64, early, pltpu.roll(late, 64, 1))
        out[1, :, lanes] = jnp.where(lane < 64, pltpu.roll(early, 64, 1), late)

    def product(place, sub):
        core_wait(place, sub)
        n = place * 2 + sub
        for tile in (1, 0):
            for k in range(8):
                block = info_s[0, k] if tile else sources[0, k]
                columns[:, k * 256 : k * 256 + 256] = gathered[place][sub][(block % 2) * 8 + block // 2]
            result = lax.dot_general(
                wide[tile], columns[...], (((1,), (1,)), ((), ())), preferred_element_type=F32
            )
            if tile:
                sent_tiles[n] = result.astype(BF16)
                start(tile_copy(n))
            elif sub == 0:
                held[place] = result
            else:
                place_tile(held[place], result, xh, place)

    relay(0)
    info_copy.wait()
    listed = pltpu.make_async_copy(info_got, info_s, local_sem.at[2])
    listed.start()
    listed.wait()
    for step in (1, 2, 3):
        maty_wait(step)
    other_live = info_s[1, 0]
    for k in range(8):
        wide[1, :, k * 256 : k * 256 + 256] = other_mat[k] * jnp.where(k < other_live, 1.0, 0.0).astype(BF16)
    product(0, 0)
    product(0, 1)
    relay(1)
    product(1, 0)
    product(2, 0)
    far(0)
    product(1, 1)
    product(2, 1)
    far(1)
    product(3, 0)
    product(3, 1)
    for place in range(4):
        for sub in range(SUBS):
            tile_copy(place * 2 + sub).wait_recv()
        place_tile(got_tiles[place * 2].astype(F32), got_tiles[place * 2 + 1].astype(F32), 1 - xh, place)

    for copy in pending:
        copy.wait_send()
    for step in (1, 2, 3):
        pary_copy(step).wait_send()
        maty_copy(step).wait_send()
    mat_copy.wait_send()

    def wait_sent(step, carry):
        for sub in range(SUBS):
            child_copy(sub, step, a).wait_send()
        return carry

    lax.fori_loop(1, 16, wait_sent, 0)

    def wait_par_sent(step, carry):
        par_copy(step, me).wait_send()
        return carry

    lax.fori_loop(1, 8, wait_par_sent, 0)


def shards(child, taps, bands, shifts, bases, slopes, sources, counts, matrices):
    counts = counts.reshape(1, 1)
    matrices = matrices[0]
    vmem = pl.BlockSpec(memory_space=pltpu.VMEM)
    smem = pl.BlockSpec(memory_space=pltpu.SMEM)
    dma = pltpu.SemaphoreType.DMA
    scratch = [
        pltpu.VMEM((16, 2, TILES, 2, 8, 128), F32),
        pltpu.VMEM((2, 2, 2, 8, 128), F32),
        pltpu.VMEM((SUBS, 16, TILES, 2, 8, 128), F32),
        pltpu.VMEM((2, 16, TILES * 16, 256), BF16),
        pltpu.VMEM((2, TILES * 16, 256), F32),
        pltpu.VMEM((64, 256, 256), BF16),
        pltpu.VMEM((64, 2, 8, 256), F32),
        pltpu.VMEM((64, 8, 256), F32),
        pltpu.VMEM((4, 16, 256), F32),
        pltpu.VMEM((4, 8, 16, 256), F32),
        *[pltpu.VMEM((16, 128, 256), BF16) for _ in range(8)],
        pltpu.VMEM((8, 512, 256), BF16),
        pltpu.VMEM((2, 512, 2048), BF16),
        pltpu.VMEM((128, 2048), BF16),
        pltpu.VMEM((8, 512, 128), BF16),
        pltpu.VMEM((8, 512, 128), BF16),
        pltpu.VMEM((4, 512, 128), F32),
        pltpu.VMEM((8, 128), jnp.int32),
        pltpu.VMEM((8, 128), jnp.int32),
        pltpu.SMEM((8, 128), jnp.int32),
        dma((2, 16)), dma((2, 16)),
        dma((2,)), dma((2,)),
        dma((8,)), dma((8,)),
        dma((4,)), dma((4,)),
        dma((1,)), dma((1,)),
        dma((4,)), dma((4,)),
        dma((4,)), dma((4,)),
        dma((4,)), dma((4,)),
        dma((8,)), dma((8,)),
        dma((8,)), dma((8,)),
        dma((1,)), dma((1,)),
        dma((3,)),
    ]
    return pl.pallas_call(
        kernel,
        out_shape=jax.ShapeDtypeStruct((2, 512, 1024), F32),
        in_specs=[vmem] * 9 + [smem] * 2,
        out_specs=vmem,
        scratch_shapes=scratch,
        compiler_params=pltpu.CompilerParams(
            collective_id=0, has_side_effects=True, vmem_limit_bytes=62 * 2**20
        ),
    )(child, taps, bands, shifts, bases, slopes, sources, counts, matrices, sources, counts)


def solution(mesh):
    placed = (
        P(None, "aperture", "range"),
        P(None, None, None, "aperture"),
        P(None, None, "aperture"),
        P(None, None, "aperture"),
        P(None, None, "aperture"),
        P(None, None, "aperture"),
        P("aperture", None),
        P("aperture"),
        P("aperture", None, None, None),
    )
    return jax.shard_map(
        shards, mesh=mesh, in_specs=placed, out_specs=P(None, "aperture", "range"), check_vma=False
    )
```

```python
import functools

import jax
import jax.numpy as jnp
import numpy as np
from jax import lax
from jax.experimental import pallas as pl
from jax.experimental.pallas import tpu as pltpu
from jax.sharding import PartitionSpec as P

RANGE = 8192
SCALE = 0.70710678
MESH = pl.DeviceIdType.MESH
SUBS = 2
ROWS = 64
TILES = 9
F32 = jnp.float32
BF16 = jnp.bfloat16


def turn_by(angle):
    quarters = jnp.round(angle * (2.0 / np.pi))
    x = angle - quarters * 1.5703125
    x = x - quarters * 4.838267948966e-4
    x2 = x * x
    sine = x + x * x2 * (-1.6666654611e-1 + x2 * (8.3321608736e-3 - x2 * 1.9515295891e-4))
    cosine = 1.0 - 0.5 * x2 + x2 * x2 * (4.166664568298827e-2 + x2 * (-1.388731625493765e-3 + x2 * 2.443315711809948e-5))
    part = quarters - 4.0 * jnp.floor(quarters * 0.25)
    odd = (part == 1.0) | (part == 3.0)
    first = jnp.where(odd, sine, cosine)
    second = jnp.where(odd, cosine, sine)
    first = jnp.where((part == 1.0) | (part == 2.0), -first, first)
    second = jnp.where(part >= 2.0, -second, second)
    return first, second


def kernel(
    child_h, taps, bands, shifts, bases, slopes, sources_v, counts_v, matrices, sources, counts,
    out,
    child, own_mat, staged, edges, coded, received, split, part, bank, wave, rates, own_par, par,
    g00, g01, g10, g11, g20, g21, g30, g31,
    other_mat, wide, columns, sent_tiles, got_tiles, held, info, info_got, info_s,
    a2a_send, a2a_recv, edge_send, edge_recv, par_send, par_recv, pary_send, pary_recv,
    mat_send, mat_recv, maty_send, maty_recv, ring_send, ring_recv, relay_send, relay_recv,
    core_send, core_recv, tile_send, tile_recv, info_send, info_recv, local_sem,
):
    gathered = ((g00, g01), (g10, g11), (g20, g21), (g30, g31))
    a = lax.axis_index("aperture")
    p = lax.axis_index("range")
    core, z, xh = a % 2, (a // 2) % 4, a // 8
    y, xl = p // 2, p % 2
    me = a // 2
    sibling = (me * 2 + 1 - core, p)
    z_next = (xh * 8 + ((z + 1) % 4) * 2 + core, p)
    z_prev = (xh * 8 + ((z + 3) % 4) * 2 + core, p)
    x_pair = ((a + 8) % 16, p)
    x_side = ((a + 8) % 16, y * 2 + 1 - xl)
    r_next = (a, (p + 1) % 8)
    r_prev = (a, (p + 7) % 8)

    def y_peer(step):
        return (a, ((y + step) % 4) * 2 + xl)

    load_child = pltpu.make_async_copy(child_h, child, local_sem.at[3])
    load_child.start()
    load_mat = pltpu.make_async_copy(matrices, own_mat, local_sem.at[4])
    load_mat.start()

    barrier = pltpu.get_barrier_semaphore()

    def greet(step, carry):
        pl.semaphore_signal(barrier, inc=1, device_id=((a + step) % 16, p), device_id_type=MESH)
        return carry

    lax.fori_loop(1, 16, greet, 0)
    for peer in (x_side, r_next, r_prev, y_peer(1), y_peer(2), y_peer(3)):
        pl.semaphore_signal(barrier, inc=1, device_id=peer, device_id_type=MESH)

    for level in range(4):
        for side in range(2):
            row = side * 8
            own_par[level, row : row + 4, :] = taps[level, side]
            own_par[level, row + 4 : row + 5, :] = bands[level, side : side + 1, :].astype(F32)
            own_par[level, row + 5 : row + 6, :] = shifts[level, side : side + 1, :]
            own_par[level, row + 6 : row + 7, :] = bases[level, side : side + 1, :]
            own_par[level, row + 7 : row + 8, :] = slopes[level, side : side + 1, :]
    info[...] = jnp.zeros((8, 128), jnp.int32)
    info[0:1, 0:8] = sources_v[...]
    info[1:2, 0:1] = counts_v[...]

    load_child.wait()

    def turn(k, carry):
        for comp in range(2):
            for half in range(2):
                block = child[comp, half * 128 : half * 128 + 128, pl.ds(pl.multiple_of(k * 128, 128), 128)]
                block = block.T.reshape(2, 8, 8, 128)
                for sub in range(2):
                    staged[k * 2 + sub, half, 0:8, comp] = block[sub]
        return carry

    lax.fori_loop(0, 8, turn, 0)

    pl.semaphore_wait(barrier, 21)

    def remote(src, dst, send, recv, to):
        return pltpu.make_async_remote_copy(
            src_ref=src, dst_ref=dst, send_sem=send, recv_sem=recv, device_id=to, device_id_type=MESH
        )

    there = p + 1 - 2 * (p % 2)

    def mat_first(n):
        return remote(
            matrices.at[pl.ds(n, 1)], other_mat.at[pl.ds(n, 1)], mat_send.at[0], mat_recv.at[0], x_side
        )

    def mat_second(n):
        return remote(
            other_mat.at[pl.ds(n, 1)], other_mat.at[pl.ds(n, 1)], mat_send.at[1], mat_recv.at[1], (a, there)
        )

    mat_first(p).start()

    def par_copy(step, slot):
        return remote(
            own_par.at[y], par.at[y, slot], par_send.at[step], par_recv.at[slot], ((a + 2 * step) % 16, p)
        )

    def send_par(step, carry):
        par_copy(step, me).start()
        return carry

    lax.fori_loop(1, 8, send_par, 0)
    info_copy = remote(info, info_got, info_send.at[0], info_recv.at[0], x_pair)
    info_copy.start()

    edge_next = remote(staged.at[15, :, 7], edges.at[0], edge_send.at[0], edge_recv.at[0], r_next)
    edge_prev = remote(staged.at[0, :, 0], edges.at[1], edge_send.at[1], edge_recv.at[1], r_prev)
    edge_next.start()
    edge_prev.start()
    low = lax.broadcasted_iota(jnp.int32, (8, 128), 0) < 4

    def fill(j, carry):
        for half in range(2):
            for comp in range(2):
                staged[j, half, 8, comp] = jnp.where(low, staged[j + 1, half, 0, comp], staged[j - 1, half, 7, comp])
        return carry

    def code(j, carry):
        for half in range(2):
            x = staged[j, half].reshape(TILES * 16, 128)
            most = jnp.max(jnp.abs(x), axis=0, keepdims=True)
            power = jnp.ceil(jnp.log2(jnp.maximum(most, 1e-30)) - 14.9999)
            coded[j, half, 0 : TILES * 16] = jnp.round(x * jnp.exp2(-power)).astype(jnp.int16)
            coded[j, half, TILES * 16 : TILES * 16 + 16] = jnp.broadcast_to(power, (16, 128)).astype(jnp.int16)
        return carry

    def fill_code(j, carry):
        return code(j, fill(j, carry))

    def child_copy(sub, step, slot):
        to = (a + step) % 16
        return remote(
            coded.at[(to // 2) * 2 + sub, to % 2],
            received.at[sub, slot],
            a2a_send.at[sub, step],
            a2a_recv.at[sub, slot],
            (to, p),
        )

    def keep_copy(sub):
        return pltpu.make_async_copy(coded.at[me * 2 + sub, core], received.at[sub, a], local_sem.at[sub])

    def send_children(sub, edge):
        last = 7 * sub

        def send_child(step, carry):
            @pl.when((((a + step) % 16) // 2 == last) == edge)
            def _():
                child_copy(sub, step, a).start()

            return carry

        lax.fori_loop(1, 16, send_child, 0)

        @pl.when((me == last) == edge)
        def _():
            keep_copy(sub).start()

    lax.fori_loop(1, 15, fill_code, 0)
    send_children(0, False)
    edge_next.wait()
    edge_prev.wait()
    has_prev = jnp.where(p > 0, 1.0, 0.0).astype(F32)
    has_next = jnp.where(p < 7, 1.0, 0.0).astype(F32)
    for half in range(2):
        for comp in range(2):
            staged[0, half, 8, comp] = jnp.where(low, staged[1, half, 0, comp], edges[0, half, comp] * has_prev)
            staged[15, half, 8, comp] = jnp.where(low, edges[1, half, comp] * has_next, staged[14, half, 7, comp])
    code(0, 0)
    code(15, 0)
    send_children(0, True)

    par[y, me] = own_par[y]

    def wait_par(step, carry):
        par_copy(step, (me + step) % 8).wait_recv()
        return carry

    lax.fori_loop(1, 8, wait_par, 0)

    def pary_copy(step):
        return remote(par.at[y], par.at[y], pary_send.at[step], pary_recv.at[step], y_peer(step))

    def pary_wait(step):
        there = (y + 4 - step) % 4
        remote(par.at[there], par.at[there], pary_send.at[step], pary_recv.at[step], y_peer(step)).wait_recv()

    for step in (1, 2, 3):
        pary_copy(step).start()

    def maty_copy(piece, step):
        own = pl.ds((there, p)[piece], 1)
        n = piece * 4 + step
        return remote(other_mat.at[own], other_mat.at[own], maty_send.at[n], maty_recv.at[n], y_peer(step))

    def maty_wait(piece, step):
        p_far = ((y + 4 - step) % 4) * 2 + xl
        far = pl.ds((p_far + 1 - 2 * (p_far % 2), p_far)[piece], 1)
        n = piece * 4 + step
        remote(other_mat.at[far], other_mat.at[far], maty_send.at[n], maty_recv.at[n], y_peer(step)).wait_recv()

    mat_first(there).wait_recv()
    for step in (1, 3, 2):
        maty_copy(0, step).start()
    mat_second(there).start()

    load_mat.wait()
    live = counts[0, 0]
    for k in range(8):
        wide[0, :, k * 256 : k * 256 + 256] = own_mat[k] * jnp.where(k < live, 1.0, 0.0).astype(BF16)

    def wait_sent(step, carry):
        child_copy(0, step, a).wait_send()
        return carry

    lax.fori_loop(1, 16, wait_sent, 0)
    send_children(1, False)
    send_children(1, True)
    for step in (1, 2, 3):
        pary_wait(step)
    mat_second(p).wait_recv()
    for step in (1, 3, 2):
        maty_copy(1, step).start()

    first = p * 1024 + me * (SUBS * ROWS)
    beam = lax.broadcasted_iota(jnp.int32, (128, 256), 0).astype(F32).astype(BF16)
    radius = (first + lax.broadcasted_iota(jnp.int32, (8, 256), 0)).astype(F32) * (1.0 / RANGE)
    for level in range(4):

        def prepare(q, carry, level=level):
            half = core if level == 0 else (q // (1 << (level - 1))) % 2
            start = (half * 128).astype(F32)
            for side in range(2):
                index = (level * 8 + q) * 2 + side
                rows = par[level, q, side * 8 : side * 8 + 8, :]
                place = rows[4:5] - start
                weight = rows[0:4]
                high = weight.astype(BF16)
                rest = (weight - high.astype(F32)).astype(BF16)
                tops = jnp.zeros((128, 256), BF16)
                tails = jnp.zeros((128, 256), BF16)
                for tap in range(4):
                    hit = beam == (place + float(tap)).astype(BF16)
                    tops = jnp.where(hit, high[tap : tap + 1], tops)
                    tails = jnp.where(hit, rest[tap : tap + 1], tails)
                bank[index, 0:128] = tops
                bank[index, 128:256] = tails
                cosine, sine = turn_by(rows[6:7] + rows[7:8] * radius)
                wave[index, 0] = SCALE * cosine
                wave[index, 1] = SCALE * sine
                step = rows[7:8] * (8.0 / RANGE)
                step2 = step * step
                rates[index, 0:1] = 1.0 - 0.5 * step2 + step2 * step2 * (1.0 / 24.0)
                rates[index, 1:2] = step - step * step2 * (1.0 / 6.0)
                rates[index, 2:3] = jnp.abs(rows[5:6])
                rates[index, 3:4] = rows[5:6]
            return carry

        lax.fori_loop(0, 8, prepare, 0)

    row8 = lax.broadcasted_iota(jnp.int32, (8, 128), 0)

    def run_level(level, sub):
        source, target = split.at[level % 2], split.at[(level + 1) % 2]
        start = first + sub * ROWS
        bins = start + jnp.where(low, ROWS + row8, row8 - 8)
        inside = jnp.where((bins >= 0) & (bins < RANGE), 1.0, 0.0).astype(F32)

        def one(q, carry):
            index = (level * 8 + q) * 2
            for side in range(2):
                if level == 0:
                    slot = 2 * q + side
                else:
                    bit = 1 << (level - 1)
                    half = (q // bit) % 2
                    slot = (q - half * bit + side * bit) * 2 + half
                x = source[slot]
                w = bank[index + side]
                high, rest = w[0:128], w[128:256]
                part[side] = jnp.dot(
                    jnp.concatenate([x, x], axis=1),
                    jnp.concatenate([high, high, rest, rest], axis=0),
                    preferred_element_type=F32,
                )
            for half in range(2):
                lanes = slice(half * 128, half * 128 + 128)

                def load(side, comp, t):
                    return part[side, t * 16 + comp * 8 : t * 16 + comp * 8 + 8, lanes]

                cosine = [wave[index + s, 0, :, lanes] for s in range(2)]
                sine = [wave[index + s, 1, :, lanes] for s in range(2)]
                step_c = [jnp.broadcast_to(rates[index + s, 0:1, lanes], (8, 128)) for s in range(2)]
                step_s = [jnp.broadcast_to(rates[index + s, 1:2, lanes], (8, 128)) for s in range(2)]
                amount = [jnp.broadcast_to(rates[index + s, 2:3, lanes], (8, 128)) for s in range(2)]
                ahead = [jnp.broadcast_to(rates[index + s, 3:4, lanes], (8, 128)) > 0.0 for s in range(2)]
                back_c = [cosine[s] * step_c[s] + sine[s] * step_s[s] for s in range(2)]
                back_s = [sine[s] * step_c[s] - cosine[s] * step_s[s] for s in range(2)]
                up, down = {}, {}
                for s in range(2):
                    for comp in range(2):
                        up[s, comp, 0] = pltpu.roll(load(s, comp, 0), 7, 0)
                        down[s, comp, -1] = pltpu.roll(load(s, comp, TILES - 1), 1, 0)
                previous = None
                for t in range(TILES if level < 3 else TILES - 1):
                    if t == TILES - 1:
                        if sub + 1 < SUBS:
                            for s in range(2):
                                wave[index + s, 0, :, lanes] = cosine[s]
                                wave[index + s, 1, :, lanes] = sine[s]
                        for s in range(2):
                            cosine[s] = jnp.where(low, cosine[s], back_c[s])
                            sine[s] = jnp.where(low, sine[s], back_s[s])
                    total = [None, None]
                    for s in range(2):
                        moved = []
                        for comp in range(2):
                            center = load(s, comp, t)
                            if t + 1 < TILES:
                                up[s, comp, t + 1] = pltpu.roll(load(s, comp, t + 1), 7, 0)
                                following = up[s, comp, t + 1]
                            else:
                                following = pltpu.roll(load(s, comp, 0), 7, 0)
                            down[s, comp, t] = pltpu.roll(center, 1, 0)
                            after = jnp.where(row8 == 7, following, up[s, comp, t])
                            before = jnp.where(row8 == 0, down[s, comp, t - 1], down[s, comp, t])
                            beside = jnp.where(ahead[s], after, before)
                            moved.append(center + amount[s] * (beside - center))
                        real = moved[0] * cosine[s] - moved[1] * sine[s]
                        imag = moved[0] * sine[s] + moved[1] * cosine[s]
                        total = [real, imag] if s == 0 else [total[0] + real, total[1] + imag]
                        if t < TILES - 1:
                            cosine[s], sine[s] = (
                                cosine[s] * step_c[s] - sine[s] * step_s[s],
                                sine[s] * step_c[s] + cosine[s] * step_s[s],
                            )
                    if level < 3:
                        if t == TILES - 1:
                            total = [v * inside for v in total]
                        both = jnp.concatenate(total, axis=0)
                        high = both.astype(BF16)
                        target[q * 2 + half, t * 16 : t * 16 + 16, 0:128] = high
                        target[q * 2 + half, t * 16 : t * 16 + 16, 128:256] = (both - high.astype(F32)).astype(BF16)
                    elif t % 2 == 0:
                        previous = total
                    else:
                        for comp in range(2):
                            row = comp * ROWS + (t // 2) * 16
                            gathered[0][sub][core * 8 + q, row : row + 16, lanes] = jnp.concatenate(
                                [previous[comp], total[comp]], axis=0
                            ).astype(BF16)
                if level == 3 and sub + 1 < SUBS:
                    for s in range(2):
                        wave[index + s, 0, :, lanes] = cosine[s]
                        wave[index + s, 1, :, lanes] = sine[s]
            return carry

        lax.fori_loop(0, 8, one, 0)

    own_half = pl.ds(core * 8, 8)
    pending = []

    def start(copy):
        copy.start()
        pending.append(copy)

    def core_copy(place, sub):
        ref = gathered[place][sub].at[own_half]
        n = place * 2 + sub
        return remote(ref, ref, core_send.at[n], core_recv.at[n], sibling)

    def core_wait(place, sub):
        ref = gathered[place][sub].at[pl.ds((1 - core) * 8, 8)]
        n = place * 2 + sub
        remote(ref, ref, core_send.at[n], core_recv.at[n], sibling).wait_recv()

    def ring_copy(way, sub):
        n = way * 2 + sub
        return remote(
            gathered[0][sub].at[own_half], gathered[1 + way][sub].at[own_half],
            ring_send.at[n], ring_recv.at[n], (z_next, z_prev)[way],
        )

    def relay_copy(way, sub):
        n = way * 2 + sub
        quarter = pl.ds(core * 8 + way * 4, 4)
        return remote(
            gathered[1 + way][sub].at[quarter], gathered[3][sub].at[quarter],
            relay_send.at[n], relay_recv.at[n], (z_next, z_prev)[way],
        )

    for sub in range(SUBS):

        def wait_child(step, carry, sub=sub):
            child_copy(sub, step, (a + step) % 16).wait_recv()
            return carry

        lax.fori_loop(1, 16, wait_child, 0)
        keep_copy(sub).wait()

        def halve(n, carry, sub=sub):
            power = received[sub, n, TILES * 16 : TILES * 16 + 16].astype(F32)[0:1]
            x = received[sub, n, 0 : TILES * 16].astype(F32) * jnp.exp2(power)
            high = x.astype(BF16)
            split[0, n, :, 0:128] = high
            split[0, n, :, 128:256] = (x - high.astype(F32)).astype(BF16)
            return carry

        lax.fori_loop(0, 16, halve, 0)
        for level in range(4):
            run_level(level, sub)
        for way in range(2):
            start(ring_copy(way, sub))
        start(core_copy(0, sub))

    def relay(sub):
        for way in range(2):
            ring_copy(way, sub).wait_recv()
            start(relay_copy(way, sub))
            start(core_copy(1 + way, sub))

    def far(sub):
        for way in range(2):
            relay_copy(way, sub).wait_recv()
        start(core_copy(3, sub))

    def tile_copy(n):
        return remote(sent_tiles.at[n], got_tiles.at[n], tile_send.at[n], tile_recv.at[n], x_pair)

    lane = lax.broadcasted_iota(jnp.int32, (512, 128), 1)

    def place_tile(early, late, side, place):
        where = (side * 4 + (z + (0, 3, 1, 2)[place]) % 4) * 128
        lanes = pl.ds(pl.multiple_of(where, 128), 128)
        out[0, :, lanes] = jnp.where(lane < 64, early, pltpu.roll(late, 64, 1))
        out[1, :, lanes] = jnp.where(lane < 64, pltpu.roll(early, 64, 1), late)

    def product(place, sub, tile):
        n = place * 2 + sub
        for k in range(8):
            block = info_s[0, k] if tile else sources[0, k]
            columns[:, k * 256 : k * 256 + 256] = gathered[place][sub][(block % 2) * 8 + block // 2]
        result = lax.dot_general(
            wide[tile], columns[...], (((1,), (1,)), ((), ())), preferred_element_type=F32
        )
        if tile:
            sent_tiles[n] = result.astype(BF16)
            start(tile_copy(n))
        elif sub == 0:
            held[place] = result
        else:
            place_tile(held[place], result, xh, place)

    for sub in range(SUBS):
        core_wait(0, sub)
        product(0, sub, 0)
    relay(0)
    info_copy.wait()
    listed = pltpu.make_async_copy(info_got, info_s, local_sem.at[2])
    listed.start()
    listed.wait()
    for piece in range(2):
        for step in (1, 2, 3):
            maty_wait(piece, step)
    other_live = info_s[1, 0]
    for k in range(8):
        wide[1, :, k * 256 : k * 256 + 256] = other_mat[k] * jnp.where(k < other_live, 1.0, 0.0).astype(BF16)
    product(0, 0, 1)
    product(0, 1, 1)

    def both(place, sub):
        core_wait(place, sub)
        product(place, sub, 1)
        product(place, sub, 0)

    both(1, 0)
    both(2, 0)
    relay(1)
    far(0)
    both(1, 1)
    both(2, 1)
    far(1)
    both(3, 0)
    both(3, 1)
    for place in range(4):
        for sub in range(SUBS):
            tile_copy(place * 2 + sub).wait_recv()
        place_tile(got_tiles[place * 2].astype(F32), got_tiles[place * 2 + 1].astype(F32), 1 - xh, place)

    for copy in pending:
        copy.wait_send()
    for step in (1, 2, 3):
        pary_copy(step).wait_send()
        for piece in range(2):
            maty_copy(piece, step).wait_send()
    mat_first(p).wait_send()
    mat_second(there).wait_send()

    def wait_last_sent(step, carry):
        child_copy(1, step, a).wait_send()
        return carry

    lax.fori_loop(1, 16, wait_last_sent, 0)

    def wait_par_sent(step, carry):
        par_copy(step, me).wait_send()
        return carry

    lax.fori_loop(1, 8, wait_par_sent, 0)


def shards(child, taps, bands, shifts, bases, slopes, sources, counts, matrices):
    counts = counts.reshape(1, 1)
    matrices = matrices[0]
    vmem = pl.BlockSpec(memory_space=pltpu.VMEM)
    smem = pl.BlockSpec(memory_space=pltpu.SMEM)
    hbm = pl.BlockSpec(memory_space=pl.ANY)
    dma = pltpu.SemaphoreType.DMA
    scratch = [
        pltpu.VMEM((2, 256, 1024), F32),
        pltpu.VMEM((8, 512, 256), BF16),
        pltpu.VMEM((16, 2, TILES, 2, 8, 128), F32),
        pltpu.VMEM((2, 2, 2, 8, 128), F32),
        pltpu.VMEM((16, 2, TILES * 16 + 16, 128), jnp.int16),
        pltpu.VMEM((SUBS, 16, TILES * 16 + 16, 128), jnp.int16),
        pltpu.VMEM((2, 16, TILES * 16, 256), BF16),
        pltpu.VMEM((2, TILES * 16, 256), F32),
        pltpu.VMEM((64, 256, 256), BF16),
        pltpu.VMEM((64, 2, 8, 256), F32),
        pltpu.VMEM((64, 8, 256), F32),
        pltpu.VMEM((4, 16, 256), F32),
        pltpu.VMEM((4, 8, 16, 256), F32),
        *[pltpu.VMEM((16, 128, 256), BF16) for _ in range(8)],
        pltpu.VMEM((8, 512, 256), BF16),
        pltpu.VMEM((2, 512, 2048), BF16),
        pltpu.VMEM((128, 2048), BF16),
        pltpu.VMEM((8, 512, 128), BF16),
        pltpu.VMEM((8, 512, 128), BF16),
        pltpu.VMEM((4, 512, 128), F32),
        pltpu.VMEM((8, 128), jnp.int32),
        pltpu.VMEM((8, 128), jnp.int32),
        pltpu.SMEM((8, 128), jnp.int32),
        dma((2, 16)), dma((2, 16)),
        dma((2,)), dma((2,)),
        dma((8,)), dma((8,)),
        dma((4,)), dma((4,)),
        dma((2,)), dma((2,)),
        dma((8,)), dma((8,)),
        dma((4,)), dma((4,)),
        dma((4,)), dma((4,)),
        dma((8,)), dma((8,)),
        dma((8,)), dma((8,)),
        dma((1,)), dma((1,)),
        dma((5,)),
    ]
    return pl.pallas_call(
        kernel,
        out_shape=pltpu.VMEM((2, 512, 1024), F32),
        in_specs=[hbm] + [vmem] * 7 + [hbm] + [smem] * 2,
        out_specs=vmem,
        scratch_shapes=scratch,
        compiler_params=pltpu.CompilerParams(
            collective_id=0, has_side_effects=True, vmem_limit_bytes=56 * 2**20
        ),
    )(child, taps, bands, shifts, bases, slopes, sources, counts, matrices, sources, counts)


def solution(mesh):
    placed = (
        P(None, "aperture", "range"),
        P(None, None, None, "aperture"),
        P(None, None, "aperture"),
        P(None, None, "aperture"),
        P(None, None, "aperture"),
        P(None, None, "aperture"),
        P("aperture", None),
        P("aperture"),
        P("aperture", None, None, None),
    )
    return jax.shard_map(
        shards, mesh=mesh, in_specs=placed, out_specs=P(None, "aperture", "range"), check_vma=False
    )
```

```python
import functools

import jax
import jax.numpy as jnp
import numpy as np
from jax import lax
from jax.experimental import pallas as pl
from jax.experimental.pallas import tpu as pltpu
from jax.sharding import PartitionSpec as P

RANGE = 8192
SCALE = 0.70710678
MESH = pl.DeviceIdType.MESH
SUBS = 2
ROWS = 64
TILES = 9
F32 = jnp.float32
BF16 = jnp.bfloat16


def turn_by(angle):
    quarters = jnp.round(angle * (2.0 / np.pi))
    x = angle - quarters * 1.5703125
    x = x - quarters * 4.838267948966e-4
    x2 = x * x
    sine = x + x * x2 * (-1.6666654611e-1 + x2 * (8.3321608736e-3 - x2 * 1.9515295891e-4))
    cosine = 1.0 - 0.5 * x2 + x2 * x2 * (4.166664568298827e-2 + x2 * (-1.388731625493765e-3 + x2 * 2.443315711809948e-5))
    part = quarters - 4.0 * jnp.floor(quarters * 0.25)
    odd = (part == 1.0) | (part == 3.0)
    first = jnp.where(odd, sine, cosine)
    second = jnp.where(odd, cosine, sine)
    first = jnp.where((part == 1.0) | (part == 2.0), -first, first)
    second = jnp.where(part >= 2.0, -second, second)
    return first, second


def kernel(
    child_h, taps, bands, shifts, bases, slopes, sources_v, counts_v, matrices, sources, counts,
    out,
    child, own_mat, staged, edges, coded, received, split, part0, part1, bank, wave, rates, own_par, par,
    g00, g01, g10, g11, g20, g21, g30, g31,
    other_mat, wide, columns, sent_tiles, got_tiles, held, info, info_got, info_s,
    a2a_send, a2a_recv, edge_send, edge_recv, par_send, par_recv, pary_send, pary_recv,
    mat_send, mat_recv, maty_send, maty_recv, ring_send, ring_recv, relay_send, relay_recv,
    core_send, core_recv, tile_send, tile_recv, info_send, info_recv, local_sem,
):
    gathered = ((g00, g01), (g10, g11), (g20, g21), (g30, g31))
    a = lax.axis_index("aperture")
    p = lax.axis_index("range")
    core, z, xh = a % 2, (a // 2) % 4, a // 8
    y, xl = p // 2, p % 2
    me = a // 2
    sibling = (me * 2 + 1 - core, p)
    z_next = (xh * 8 + ((z + 1) % 4) * 2 + core, p)
    z_prev = (xh * 8 + ((z + 3) % 4) * 2 + core, p)
    x_pair = ((a + 8) % 16, p)
    x_side = ((a + 8) % 16, y * 2 + 1 - xl)
    r_next = (a, (p + 1) % 8)
    r_prev = (a, (p + 7) % 8)

    def y_peer(step):
        return (a, ((y + step) % 4) * 2 + xl)

    load_child = pltpu.make_async_copy(child_h, child, local_sem.at[3])
    load_child.start()
    load_mat = pltpu.make_async_copy(matrices, own_mat, local_sem.at[4])
    load_mat.start()

    barrier = pltpu.get_barrier_semaphore()

    def greet(step, carry):
        pl.semaphore_signal(barrier, inc=1, device_id=((a + step) % 16, p), device_id_type=MESH)
        return carry

    lax.fori_loop(1, 16, greet, 0)
    for peer in (x_side, r_next, r_prev, y_peer(1), y_peer(2), y_peer(3)):
        pl.semaphore_signal(barrier, inc=1, device_id=peer, device_id_type=MESH)

    for level in range(4):
        for side in range(2):
            row = side * 8
            own_par[level, row : row + 4, :] = taps[level, side]
            own_par[level, row + 4 : row + 5, :] = bands[level, side : side + 1, :].astype(F32)
            own_par[level, row + 5 : row + 6, :] = shifts[level, side : side + 1, :]
            own_par[level, row + 6 : row + 7, :] = bases[level, side : side + 1, :]
            own_par[level, row + 7 : row + 8, :] = slopes[level, side : side + 1, :]
    info[...] = jnp.zeros((8, 128), jnp.int32)
    info[0:1, 0:8] = sources_v[...]
    info[1:2, 0:1] = counts_v[...]

    load_child.wait()

    def turn(k, carry):
        for comp in range(2):
            for half in range(2):
                block = child[comp, half * 128 : half * 128 + 128, pl.ds(pl.multiple_of(k * 128, 128), 128)]
                block = block.T.reshape(2, 8, 8, 128)
                for sub in range(2):
                    staged[k * 2 + sub, half, 0:8, comp] = block[sub]
        return carry

    lax.fori_loop(0, 8, turn, 0)

    pl.semaphore_wait(barrier, 21)

    def remote(src, dst, send, recv, to):
        return pltpu.make_async_remote_copy(
            src_ref=src, dst_ref=dst, send_sem=send, recv_sem=recv, device_id=to, device_id_type=MESH
        )

    there = p + 1 - 2 * (p % 2)

    def mat_first(n, part):
        where = other_mat.at[pl.ds(n, 1), part * 64 : part * 64 + 64]
        return remote(
            matrices.at[pl.ds(n, 1), part * 64 : part * 64 + 64], where, mat_send.at[part], mat_recv.at[part], x_side
        )

    def mat_second(n, part):
        where = other_mat.at[pl.ds(n, 1), part * 64 : part * 64 + 64]
        return remote(where, where, mat_send.at[8 + part], mat_recv.at[8 + part], (a, there))

    def par_copy(step, slot):
        return remote(
            own_par.at[y], par.at[y, slot], par_send.at[step], par_recv.at[slot], ((a + 2 * step) % 16, p)
        )

    def send_par(step, carry):
        par_copy(step, me).start()
        return carry

    lax.fori_loop(1, 8, send_par, 0)
    info_copy = remote(info, info_got, info_send.at[0], info_recv.at[0], x_pair)
    info_copy.start()
    for part in range(8):
        mat_first(p, part).start()

    edge_next = remote(staged.at[15, :, 7], edges.at[0], edge_send.at[0], edge_recv.at[0], r_next)
    edge_prev = remote(staged.at[0, :, 0], edges.at[1], edge_send.at[1], edge_recv.at[1], r_prev)
    edge_next.start()
    edge_prev.start()
    low = lax.broadcasted_iota(jnp.int32, (8, 128), 0) < 4

    def fill(j, carry):
        for half in range(2):
            for comp in range(2):
                staged[j, half, 8, comp] = jnp.where(low, staged[j + 1, half, 0, comp], staged[j - 1, half, 7, comp])
        return carry

    def code(j, carry):
        for half in range(2):
            x = staged[j, half].reshape(TILES * 16, 128)
            most = jnp.max(jnp.abs(x), axis=0, keepdims=True)
            power = jnp.ceil(jnp.log2(jnp.maximum(most, 1e-30)) - 14.9999)
            coded[j, half, 0 : TILES * 16] = jnp.round(x * jnp.exp2(-power)).astype(jnp.int16)
            coded[j, half, TILES * 16 : TILES * 16 + 16] = jnp.broadcast_to(power, (16, 128)).astype(jnp.int16)
        return carry

    def fill_code(j, carry):
        return code(j, fill(j, carry))

    def child_copy(sub, step, slot):
        to = (a + step) % 16
        return remote(
            coded.at[(to // 2) * 2 + sub, to % 2],
            received.at[sub, slot],
            a2a_send.at[sub, step],
            a2a_recv.at[sub, slot],
            (to, p),
        )

    def keep_copy(sub):
        return pltpu.make_async_copy(coded.at[me * 2 + sub, core], received.at[sub, a], local_sem.at[sub])

    def send_children(sub, edge):
        last = 7 * sub

        def send_child(step, carry):
            @pl.when((((a + step) % 16) // 2 == last) == edge)
            def _():
                child_copy(sub, step, a).start()

            return carry

        lax.fori_loop(1, 16, send_child, 0)

        @pl.when((me == last) == edge)
        def _():
            keep_copy(sub).start()

    lax.fori_loop(1, 15, fill_code, 0)
    send_children(0, False)
    edge_next.wait()
    edge_prev.wait()
    has_prev = jnp.where(p > 0, 1.0, 0.0).astype(F32)
    has_next = jnp.where(p < 7, 1.0, 0.0).astype(F32)
    for half in range(2):
        for comp in range(2):
            staged[0, half, 8, comp] = jnp.where(low, staged[1, half, 0, comp], edges[0, half, comp] * has_prev)
            staged[15, half, 8, comp] = jnp.where(low, edges[1, half, comp] * has_next, staged[14, half, 7, comp])
    code(0, 0)
    code(15, 0)
    send_children(0, True)

    par[y, me] = own_par[y]

    def wait_par(step, carry):
        par_copy(step, (me + step) % 8).wait_recv()
        return carry

    lax.fori_loop(1, 8, wait_par, 0)

    def pary_copy(step):
        return remote(par.at[y], par.at[y], pary_send.at[step], pary_recv.at[step], y_peer(step))

    def pary_wait(step):
        there = (y + 4 - step) % 4
        remote(par.at[there], par.at[there], pary_send.at[step], pary_recv.at[step], y_peer(step)).wait_recv()

    for step in (1, 2, 3):
        pary_copy(step).start()

    def maty_copy(piece, step):
        own = pl.ds((there, p)[piece], 1)
        n = piece * 4 + step
        return remote(other_mat.at[own], other_mat.at[own], maty_send.at[n], maty_recv.at[n], y_peer(step))

    def far_piece(piece, step):
        p_far = ((y + 4 - step) % 4) * 2 + xl
        return pl.ds((p_far + 1 - 2 * (p_far % 2), p_far)[piece], 1)

    def maty_wait(piece, step):
        far = far_piece(piece, step)
        n = piece * 4 + step
        remote(other_mat.at[far], other_mat.at[far], maty_send.at[n], maty_recv.at[n], y_peer(step)).wait_recv()

    def maty_relay(piece):
        step = (1, 3)[piece]
        far = far_piece(piece, step)
        n = piece * 4 + 2
        return remote(other_mat.at[far], other_mat.at[far], maty_send.at[n], maty_recv.at[n], y_peer(step))

    for part in range(8):
        mat_first(there, part).wait_recv()
        mat_second(there, part).start()
    for step in (1, 3):
        maty_copy(0, step).start()

    load_mat.wait()
    live = counts[0, 0]
    for k in range(8):
        wide[0, :, k * 256 : k * 256 + 256] = own_mat[k] * jnp.where(k < live, 1.0, 0.0).astype(BF16)

    def wait_sent(step, carry):
        child_copy(0, step, a).wait_send()
        return carry

    lax.fori_loop(1, 16, wait_sent, 0)
    send_children(1, False)
    send_children(1, True)
    for step in (1, 2, 3):
        pary_wait(step)
    for part in range(8):
        mat_second(p, part).wait_recv()
    for step in (3, 1):
        maty_copy(1, step).start()

    first = p * 1024 + me * (SUBS * ROWS)
    beam = lax.broadcasted_iota(jnp.int32, (128, 256), 0).astype(F32).astype(BF16)
    radius = (first + lax.broadcasted_iota(jnp.int32, (8, 256), 0)).astype(F32) * (1.0 / RANGE)
    for level in range(4):

        def prepare(q, carry, level=level):
            half = core if level == 0 else (q // (1 << (level - 1))) % 2
            start = (half * 128).astype(F32)
            for side in range(2):
                index = (level * 8 + q) * 2 + side
                rows = par[level, q, side * 8 : side * 8 + 8, :]
                place = rows[4:5] - start
                weight = rows[0:4]
                high = weight.astype(BF16)
                rest = (weight - high.astype(F32)).astype(BF16)
                tops = jnp.zeros((128, 256), BF16)
                tails = jnp.zeros((128, 256), BF16)
                for tap in range(4):
                    hit = beam == (place + float(tap)).astype(BF16)
                    tops = jnp.where(hit, high[tap : tap + 1], tops)
                    tails = jnp.where(hit, rest[tap : tap + 1], tails)
                bank[index, 0:128] = tops
                bank[index, 128:256] = tails
                cosine, sine = turn_by(rows[6:7] + rows[7:8] * radius)
                wave[index, 0] = SCALE * cosine
                wave[index, 1] = SCALE * sine
                step = rows[7:8] * (8.0 / RANGE)
                step2 = step * step
                rates[index, 0:1] = 1.0 - 0.5 * step2 + step2 * step2 * (1.0 / 24.0)
                rates[index, 1:2] = step - step * step2 * (1.0 / 6.0)
                rates[index, 2:3] = jnp.abs(rows[5:6])
                rates[index, 3:4] = rows[5:6]
            return carry

        lax.fori_loop(0, 8, prepare, 0)

    maty_wait(0, 1)
    maty_relay(0).start()

    row8 = lax.broadcasted_iota(jnp.int32, (8, 128), 0)

    def run_level(level, sub):
        source, target = split.at[level % 2], split.at[(level + 1) % 2]
        start = first + sub * ROWS
        bins = start + jnp.where(low, ROWS + row8, row8 - 8)
        inside = jnp.where((bins >= 0) & (bins < RANGE), 1.0, 0.0).astype(F32)

        def multiply(q, part):
            index = (level * 8 + q) * 2
            for side in range(2):
                if level == 0:
                    slot = 2 * q + side
                else:
                    bit = 1 << (level - 1)
                    half = (q // bit) % 2
                    slot = (q - half * bit + side * bit) * 2 + half
                x = source[slot]
                w = bank[index + side]
                high, rest = w[0:128], w[128:256]
                part[side] = jnp.dot(
                    jnp.concatenate([x, x[:, 0:128]], axis=1),
                    jnp.concatenate([high, high, rest], axis=0),
                    preferred_element_type=F32,
                )

        def combine(q, part):
            index = (level * 8 + q) * 2
            for half in range(2):
                lanes = slice(half * 128, half * 128 + 128)

                def load(side, comp, t):
                    return part[side, t * 16 + comp * 8 : t * 16 + comp * 8 + 8, lanes]

                cosine = [wave[index + s, 0, :, lanes] for s in range(2)]
                sine = [wave[index + s, 1, :, lanes] for s in range(2)]
                step_c = [jnp.broadcast_to(rates[index + s, 0:1, lanes], (8, 128)) for s in range(2)]
                step_s = [jnp.broadcast_to(rates[index + s, 1:2, lanes], (8, 128)) for s in range(2)]
                amount = [jnp.broadcast_to(rates[index + s, 2:3, lanes], (8, 128)) for s in range(2)]
                ahead = [jnp.broadcast_to(rates[index + s, 3:4, lanes], (8, 128)) > 0.0 for s in range(2)]
                back_c = [cosine[s] * step_c[s] + sine[s] * step_s[s] for s in range(2)]
                back_s = [sine[s] * step_c[s] - cosine[s] * step_s[s] for s in range(2)]
                up, down = {}, {}
                for s in range(2):
                    for comp in range(2):
                        up[s, comp, 0] = pltpu.roll(load(s, comp, 0), 7, 0)
                        down[s, comp, -1] = pltpu.roll(load(s, comp, TILES - 1), 1, 0)
                previous = None
                for t in range(TILES if level < 3 else TILES - 1):
                    if t == TILES - 1:
                        if sub + 1 < SUBS:
                            for s in range(2):
                                wave[index + s, 0, :, lanes] = cosine[s]
                                wave[index + s, 1, :, lanes] = sine[s]
                        for s in range(2):
                            cosine[s] = jnp.where(low, cosine[s], back_c[s])
                            sine[s] = jnp.where(low, sine[s], back_s[s])
                    total = [None, None]
                    for s in range(2):
                        moved = []
                        for comp in range(2):
                            center = load(s, comp, t)
                            if t + 1 < TILES:
                                up[s, comp, t + 1] = pltpu.roll(load(s, comp, t + 1), 7, 0)
                                following = up[s, comp, t + 1]
                            else:
                                following = pltpu.roll(load(s, comp, 0), 7, 0)
                            down[s, comp, t] = pltpu.roll(center, 1, 0)
                            after = jnp.where(row8 == 7, following, up[s, comp, t])
                            before = jnp.where(row8 == 0, down[s, comp, t - 1], down[s, comp, t])
                            beside = jnp.where(ahead[s], after, before)
                            moved.append(center + amount[s] * (beside - center))
                        real = moved[0] * cosine[s] - moved[1] * sine[s]
                        imag = moved[0] * sine[s] + moved[1] * cosine[s]
                        total = [real, imag] if s == 0 else [total[0] + real, total[1] + imag]
                        if t < TILES - 1:
                            cosine[s], sine[s] = (
                                cosine[s] * step_c[s] - sine[s] * step_s[s],
                                sine[s] * step_c[s] + cosine[s] * step_s[s],
                            )
                    if level < 3:
                        if t == TILES - 1:
                            total = [v * inside for v in total]
                        both = jnp.concatenate(total, axis=0)
                        high = both.astype(BF16)
                        target[q * 2 + half, t * 16 : t * 16 + 16, 0:128] = high
                        target[q * 2 + half, t * 16 : t * 16 + 16, 128:256] = (both - high.astype(F32)).astype(BF16)
                    elif t % 2 == 0:
                        previous = total
                    else:
                        for comp in range(2):
                            row = comp * ROWS + (t // 2) * 16
                            gathered[0][sub][core * 8 + q, row : row + 16, lanes] = jnp.concatenate(
                                [previous[comp], total[comp]], axis=0
                            ).astype(BF16)
                if level == 3 and sub + 1 < SUBS:
                    for s in range(2):
                        wave[index + s, 0, :, lanes] = cosine[s]
                        wave[index + s, 1, :, lanes] = sine[s]

        def two(pair, carry):
            multiply(2 * pair + 1, part1)
            combine(2 * pair, part0)
            multiply((2 * pair + 2) % 8, part0)
            combine(2 * pair + 1, part1)
            return carry

        multiply(0, part0)
        lax.fori_loop(0, 4, two, 0)

    own_half = pl.ds(core * 8, 8)
    pending = []

    def start(copy):
        copy.start()
        pending.append(copy)

    def core_copy(place, sub):
        ref = gathered[place][sub].at[own_half]
        n = place * 2 + sub
        return remote(ref, ref, core_send.at[n], core_recv.at[n], sibling)

    def core_wait(place, sub):
        if place == 3:
            for way in range(2):
                core_far(way, sub, 1 - core).wait_recv()
            return
        ref = gathered[place][sub].at[pl.ds((1 - core) * 8, 8)]
        n = place * 2 + sub
        remote(ref, ref, core_send.at[n], core_recv.at[n], sibling).wait_recv()

    def core_far(way, sub, side=core):
        ref = gathered[3][sub].at[pl.ds(side * 8 + way * 4, 4)]
        n = 6 + sub if way == 0 else 8 + sub
        return remote(ref, ref, core_send.at[n], core_recv.at[n], sibling)

    def ring_copy(way, sub):
        n = way * 2 + sub
        return remote(
            gathered[0][sub].at[own_half], gathered[1 + way][sub].at[own_half],
            ring_send.at[n], ring_recv.at[n], (z_next, z_prev)[way],
        )

    def relay_copy(way, sub):
        n = way * 2 + sub
        quarter = pl.ds(core * 8 + way * 4, 4)
        return remote(
            gathered[1 + way][sub].at[quarter], gathered[3][sub].at[quarter],
            relay_send.at[n], relay_recv.at[n], (z_next, z_prev)[way],
        )

    for sub in range(SUBS):

        def wait_child(step, carry, sub=sub):
            child_copy(sub, step, (a + step) % 16).wait_recv()
            return carry

        lax.fori_loop(1, 16, wait_child, 0)
        keep_copy(sub).wait()

        def halve(n, carry, sub=sub):
            power = received[sub, n, TILES * 16 : TILES * 16 + 16].astype(F32)[0:1]
            x = received[sub, n, 0 : TILES * 16].astype(F32) * jnp.exp2(power)
            high = x.astype(BF16)
            split[0, n, :, 0:128] = high
            split[0, n, :, 128:256] = (x - high.astype(F32)).astype(BF16)
            return carry

        lax.fori_loop(0, 16, halve, 0)
        for level in range(4):
            run_level(level, sub)
        for way in range(2):
            start(ring_copy(way, sub))
        start(core_copy(0, sub))
        if sub == 0:
            maty_wait(1, 3)
            maty_relay(1).start()

    def relay(sub):
        for way in range(2):
            ring_copy(way, sub).wait_recv()
            start(relay_copy(way, sub))
            start(core_copy(1 + way, sub))

    def far(sub):
        for way in range(2):
            relay_copy(way, sub).wait_recv()
            start(core_far(way, sub))

    def tile_copy(n):
        return remote(sent_tiles.at[n], got_tiles.at[n], tile_send.at[n], tile_recv.at[n], x_pair)

    lane = lax.broadcasted_iota(jnp.int32, (512, 128), 1)

    def place_tile(early, late, side, place):
        where = (side * 4 + (z + (0, 3, 1, 2)[place]) % 4) * 128
        lanes = pl.ds(pl.multiple_of(where, 128), 128)
        out[0, :, lanes] = jnp.where(lane < 64, early, pltpu.roll(late, 64, 1))
        out[1, :, lanes] = jnp.where(lane < 64, pltpu.roll(early, 64, 1), late)

    def product(place, sub, tile):
        n = place * 2 + sub
        for k in range(8):
            block = info_s[0, k] if tile else sources[0, k]
            columns[:, k * 256 : k * 256 + 256] = gathered[place][sub][(block % 2) * 8 + block // 2]
        result = lax.dot_general(
            wide[tile], columns[...], (((1,), (1,)), ((), ())), preferred_element_type=F32
        )
        if tile:
            sent_tiles[n] = result.astype(BF16)
            start(tile_copy(n))
        elif sub == 0:
            held[place] = result
        else:
            place_tile(held[place], result, xh, place)

    for sub in range(SUBS):
        core_wait(0, sub)
        product(0, sub, 0)
    relay(0)
    info_copy.wait()
    listed = pltpu.make_async_copy(info_got, info_s, local_sem.at[2])
    listed.start()
    listed.wait()
    for piece, step in ((0, 3), (0, 2), (1, 1), (1, 2)):
        maty_wait(piece, step)
    other_live = info_s[1, 0]
    for k in range(8):
        wide[1, :, k * 256 : k * 256 + 256] = other_mat[k] * jnp.where(k < other_live, 1.0, 0.0).astype(BF16)
    product(0, 0, 1)
    product(0, 1, 1)

    def both(place, sub):
        core_wait(place, sub)
        product(place, sub, 1)
        product(place, sub, 0)

    both(1, 0)
    both(2, 0)
    relay(1)
    far(0)
    both(1, 1)
    both(2, 1)
    far(1)
    both(3, 0)
    both(3, 1)
    for place in range(4):
        for sub in range(SUBS):
            tile_copy(place * 2 + sub).wait_recv()
        place_tile(got_tiles[place * 2].astype(F32), got_tiles[place * 2 + 1].astype(F32), 1 - xh, place)

    for copy in pending:
        copy.wait_send()
    for step in (1, 2, 3):
        pary_copy(step).wait_send()
        for piece in range(2):
            (maty_relay(piece) if step == 2 else maty_copy(piece, step)).wait_send()
    for part in range(8):
        mat_first(p, part).wait_send()
        mat_second(there, part).wait_send()

    def wait_last_sent(step, carry):
        child_copy(1, step, a).wait_send()
        return carry

    lax.fori_loop(1, 16, wait_last_sent, 0)

    def wait_par_sent(step, carry):
        par_copy(step, me).wait_send()
        return carry

    lax.fori_loop(1, 8, wait_par_sent, 0)


def shards(child, taps, bands, shifts, bases, slopes, sources, counts, matrices):
    counts = counts.reshape(1, 1)
    matrices = matrices[0]
    vmem = pl.BlockSpec(memory_space=pltpu.VMEM)
    smem = pl.BlockSpec(memory_space=pltpu.SMEM)
    hbm = pl.BlockSpec(memory_space=pl.ANY)
    dma = pltpu.SemaphoreType.DMA
    scratch = [
        pltpu.VMEM((2, 256, 1024), F32),
        pltpu.VMEM((8, 512, 256), BF16),
        pltpu.VMEM((16, 2, TILES, 2, 8, 128), F32),
        pltpu.VMEM((2, 2, 2, 8, 128), F32),
        pltpu.VMEM((16, 2, TILES * 16 + 16, 128), jnp.int16),
        pltpu.VMEM((SUBS, 16, TILES * 16 + 16, 128), jnp.int16),
        pltpu.VMEM((2, 16, TILES * 16, 256), BF16),
        pltpu.VMEM((2, TILES * 16, 256), F32),
        pltpu.VMEM((2, TILES * 16, 256), F32),
        pltpu.VMEM((64, 256, 256), BF16),
        pltpu.VMEM((64, 2, 8, 256), F32),
        pltpu.VMEM((64, 8, 256), F32),
        pltpu.VMEM((4, 16, 256), F32),
        pltpu.VMEM((4, 8, 16, 256), F32),
        *[pltpu.VMEM((16, 128, 256), BF16) for _ in range(8)],
        pltpu.VMEM((8, 512, 256), BF16),
        pltpu.VMEM((2, 512, 2048), BF16),
        pltpu.VMEM((128, 2048), BF16),
        pltpu.VMEM((8, 512, 128), BF16),
        pltpu.VMEM((8, 512, 128), BF16),
        pltpu.VMEM((4, 512, 128), F32),
        pltpu.VMEM((8, 128), jnp.int32),
        pltpu.VMEM((8, 128), jnp.int32),
        pltpu.SMEM((8, 128), jnp.int32),
        dma((2, 16)), dma((2, 16)),
        dma((2,)), dma((2,)),
        dma((8,)), dma((8,)),
        dma((4,)), dma((4,)),
        dma((16,)), dma((16,)),
        dma((8,)), dma((8,)),
        dma((4,)), dma((4,)),
        dma((4,)), dma((4,)),
        dma((10,)), dma((10,)),
        dma((8,)), dma((8,)),
        dma((1,)), dma((1,)),
        dma((5,)),
    ]
    return pl.pallas_call(
        kernel,
        out_shape=pltpu.VMEM((2, 512, 1024), F32),
        in_specs=[hbm] + [vmem] * 7 + [hbm] + [smem] * 2,
        out_specs=vmem,
        scratch_shapes=scratch,
        compiler_params=pltpu.CompilerParams(
            collective_id=0, has_side_effects=True, vmem_limit_bytes=56 * 2**20
        ),
    )(child, taps, bands, shifts, bases, slopes, sources, counts, matrices, sources, counts)


def solution(mesh):
    placed = (
        P(None, "aperture", "range"),
        P(None, None, None, "aperture"),
        P(None, None, "aperture"),
        P(None, None, "aperture"),
        P(None, None, "aperture"),
        P(None, None, "aperture"),
        P("aperture", None),
        P("aperture"),
        P("aperture", None, None, None),
    )
    return jax.shard_map(
        shards, mesh=mesh, in_specs=placed, out_specs=P(None, "aperture", "range"), check_vma=False
    )
```

```python
import functools

import jax
import jax.numpy as jnp
import numpy as np
from jax import lax
from jax.experimental import pallas as pl
from jax.experimental.pallas import tpu as pltpu
from jax.sharding import PartitionSpec as P

RANGE = 8192
SCALE = 0.70710678
MESH = pl.DeviceIdType.MESH
SUBS = 2
ROWS = 64
TILES = 9
F32 = jnp.float32
BF16 = jnp.bfloat16


def turn_by(angle):
    quarters = jnp.round(angle * (2.0 / np.pi))
    x = angle - quarters * 1.5703125
    x = x - quarters * 4.838267948966e-4
    x2 = x * x
    sine = x + x * x2 * (-1.6666654611e-1 + x2 * (8.3321608736e-3 - x2 * 1.9515295891e-4))
    cosine = 1.0 - 0.5 * x2 + x2 * x2 * (4.166664568298827e-2 + x2 * (-1.388731625493765e-3 + x2 * 2.443315711809948e-5))
    part = quarters - 4.0 * jnp.floor(quarters * 0.25)
    odd = (part == 1.0) | (part == 3.0)
    first = jnp.where(odd, sine, cosine)
    second = jnp.where(odd, cosine, sine)
    first = jnp.where((part == 1.0) | (part == 2.0), -first, first)
    second = jnp.where(part >= 2.0, -second, second)
    return first, second


def kernel(
    child_h, taps, bands, shifts, bases, slopes, sources_v, counts_v, matrices, sources, counts,
    out,
    child, own_mat, staged, edges, coded, received, split, part0, part1, bank, wave, rates, own_par, par,
    g00, g01, g10, g11, g20, g21, g30, g31,
    other_mat, wide, columns, sent_tiles, got_tiles, held, info, info_got, info_s,
    a2a_send, a2a_recv, edge_send, edge_recv, par_send, par_recv, pary_send, pary_recv,
    mat_send, mat_recv, maty_send, maty_recv, ring_send, ring_recv, relay_send, relay_recv,
    core_send, core_recv, tile_send, tile_recv, info_send, info_recv, local_sem,
):
    gathered = ((g00, g01), (g10, g11), (g20, g21), (g30, g31))
    a = lax.axis_index("aperture")
    p = lax.axis_index("range")
    core, z, xh = a % 2, (a // 2) % 4, a // 8
    y, xl = p // 2, p % 2
    me = a // 2
    sibling = (me * 2 + 1 - core, p)
    z_next = (xh * 8 + ((z + 1) % 4) * 2 + core, p)
    z_prev = (xh * 8 + ((z + 3) % 4) * 2 + core, p)
    x_pair = ((a + 8) % 16, p)
    x_side = ((a + 8) % 16, y * 2 + 1 - xl)
    r_next = (a, (p + 1) % 8)
    r_prev = (a, (p + 7) % 8)

    def y_peer(step):
        return (a, ((y + step) % 4) * 2 + xl)

    load_child = pltpu.make_async_copy(child_h, child, local_sem.at[3])
    load_child.start()
    load_mat = pltpu.make_async_copy(matrices, own_mat, local_sem.at[4])
    load_mat.start()

    barrier = pltpu.get_barrier_semaphore()

    def greet(step, carry):
        pl.semaphore_signal(barrier, inc=1, device_id=((a + step) % 16, p), device_id_type=MESH)
        return carry

    lax.fori_loop(1, 16, greet, 0)
    for peer in (x_side, r_next, r_prev, y_peer(1), y_peer(2), y_peer(3)):
        pl.semaphore_signal(barrier, inc=1, device_id=peer, device_id_type=MESH)

    for level in range(4):
        for side in range(2):
            row = side * 8
            own_par[level, row : row + 4, :] = taps[level, side]
            own_par[level, row + 4 : row + 5, :] = bands[level, side : side + 1, :].astype(F32)
            own_par[level, row + 5 : row + 6, :] = shifts[level, side : side + 1, :]
            own_par[level, row + 6 : row + 7, :] = bases[level, side : side + 1, :]
            own_par[level, row + 7 : row + 8, :] = slopes[level, side : side + 1, :]
    info[...] = jnp.zeros((8, 128), jnp.int32)
    info[0:1, 0:8] = sources_v[...]
    info[1:2, 0:1] = counts_v[...]

    load_child.wait()

    def turn(k, carry):
        for comp in range(2):
            for half in range(2):
                block = child[comp, half * 128 : half * 128 + 128, pl.ds(pl.multiple_of(k * 128, 128), 128)]
                block = block.T.reshape(2, 8, 8, 128)
                for sub in range(2):
                    staged[k * 2 + sub, half, 0:8, comp] = block[sub]
        return carry

    lax.fori_loop(0, 8, turn, 0)

    pl.semaphore_wait(barrier, 21)

    def remote(src, dst, send, recv, to):
        return pltpu.make_async_remote_copy(
            src_ref=src, dst_ref=dst, send_sem=send, recv_sem=recv, device_id=to, device_id_type=MESH
        )

    there = p + 1 - 2 * (p % 2)

    def mat_first(n, part):
        where = other_mat.at[pl.ds(n, 1), part * 64 : part * 64 + 64]
        return remote(
            matrices.at[pl.ds(n, 1), part * 64 : part * 64 + 64], where, mat_send.at[part], mat_recv.at[part], x_side
        )

    def mat_second(n, part):
        where = other_mat.at[pl.ds(n, 1), part * 64 : part * 64 + 64]
        return remote(where, where, mat_send.at[8 + part], mat_recv.at[8 + part], (a, there))

    def par_copy(step, slot):
        return remote(
            own_par.at[y], par.at[y, slot], par_send.at[step], par_recv.at[slot], ((a + 2 * step) % 16, p)
        )

    def send_par(step, carry):
        par_copy(step, me).start()
        return carry

    lax.fori_loop(1, 8, send_par, 0)
    info_copy = remote(info, info_got, info_send.at[0], info_recv.at[0], x_pair)
    info_copy.start()
    for part in range(8):
        mat_first(p, part).start()

    edge_next = remote(staged.at[15, :, 7], edges.at[0], edge_send.at[0], edge_recv.at[0], r_next)
    edge_prev = remote(staged.at[0, :, 0], edges.at[1], edge_send.at[1], edge_recv.at[1], r_prev)
    edge_next.start()
    edge_prev.start()
    low = lax.broadcasted_iota(jnp.int32, (8, 128), 0) < 4

    def fill(j, carry):
        for half in range(2):
            for comp in range(2):
                staged[j, half, 8, comp] = jnp.where(low, staged[j + 1, half, 0, comp], staged[j - 1, half, 7, comp])
        return carry

    def code(j, carry):
        for half in range(2):
            x = staged[j, half].reshape(TILES * 16, 128)
            most = jnp.max(jnp.abs(x), axis=0, keepdims=True)
            power = jnp.ceil(jnp.log2(jnp.maximum(most, 1e-30)) - 14.9999)
            coded[j, half, 0 : TILES * 16] = jnp.round(x * jnp.exp2(-power)).astype(jnp.int16)
            coded[j, half, TILES * 16 : TILES * 16 + 16] = jnp.broadcast_to(power, (16, 128)).astype(jnp.int16)
        return carry

    def fill_code(j, carry):
        return code(j, fill(j, carry))

    def child_copy(sub, step, slot):
        to = (a + step) % 16
        return remote(
            coded.at[(to // 2) * 2 + sub, to % 2],
            received.at[sub, slot],
            a2a_send.at[sub, step],
            a2a_recv.at[sub, slot],
            (to, p),
        )

    def keep_copy(sub):
        return pltpu.make_async_copy(coded.at[me * 2 + sub, core], received.at[sub, a], local_sem.at[sub])

    def send_children(sub, edge):
        last = 7 * sub

        def send_child(step, carry):
            @pl.when((((a + step) % 16) // 2 == last) == edge)
            def _():
                child_copy(sub, step, a).start()

            return carry

        lax.fori_loop(1, 16, send_child, 0)

        @pl.when((me == last) == edge)
        def _():
            keep_copy(sub).start()

    lax.fori_loop(1, 15, fill_code, 0)
    send_children(0, False)
    edge_next.wait()
    edge_prev.wait()
    has_prev = jnp.where(p > 0, 1.0, 0.0).astype(F32)
    has_next = jnp.where(p < 7, 1.0, 0.0).astype(F32)
    for half in range(2):
        for comp in range(2):
            staged[0, half, 8, comp] = jnp.where(low, staged[1, half, 0, comp], edges[0, half, comp] * has_prev)
            staged[15, half, 8, comp] = jnp.where(low, edges[1, half, comp] * has_next, staged[14, half, 7, comp])
    code(0, 0)
    code(15, 0)
    send_children(0, True)

    par[y, me] = own_par[y]

    def wait_par(step, carry):
        par_copy(step, (me + step) % 8).wait_recv()
        return carry

    lax.fori_loop(1, 8, wait_par, 0)

    def pary_copy(step):
        return remote(par.at[y], par.at[y], pary_send.at[step], pary_recv.at[step], y_peer(step))

    def pary_wait(step):
        there = (y + 4 - step) % 4
        remote(par.at[there], par.at[there], pary_send.at[step], pary_recv.at[step], y_peer(step)).wait_recv()

    for step in (1, 2, 3):
        pary_copy(step).start()

    def maty_copy(piece, step):
        own = pl.ds((there, p)[piece], 1)
        n = piece * 4 + step
        return remote(other_mat.at[own], other_mat.at[own], maty_send.at[n], maty_recv.at[n], y_peer(step))

    def far_piece(piece, step):
        p_far = ((y + 4 - step) % 4) * 2 + xl
        return pl.ds((p_far + 1 - 2 * (p_far % 2), p_far)[piece], 1)

    def maty_wait(piece, step):
        far = far_piece(piece, step)
        n = piece * 4 + step
        remote(other_mat.at[far], other_mat.at[far], maty_send.at[n], maty_recv.at[n], y_peer(step)).wait_recv()

    def maty_relay(piece):
        step = (1, 3)[piece]
        far = far_piece(piece, step)
        n = piece * 4 + 2
        return remote(other_mat.at[far], other_mat.at[far], maty_send.at[n], maty_recv.at[n], y_peer(step))

    for part in range(8):
        mat_first(there, part).wait_recv()
        mat_second(there, part).start()
    for step in (1, 3):
        maty_copy(0, step).start()

    load_mat.wait()
    live = counts[0, 0]
    for k in range(8):
        wide[0, :, k * 256 : k * 256 + 256] = own_mat[k] * jnp.where(k < live, 1.0, 0.0).astype(BF16)

    def wait_sent(step, carry):
        child_copy(0, step, a).wait_send()
        return carry

    lax.fori_loop(1, 16, wait_sent, 0)
    send_children(1, False)
    send_children(1, True)
    for step in (1, 2, 3):
        pary_wait(step)
    for part in range(8):
        mat_second(p, part).wait_recv()
    for step in (3, 1):
        maty_copy(1, step).start()

    first = p * 1024 + me * (SUBS * ROWS)
    beam = lax.broadcasted_iota(jnp.int32, (128, 256), 0).astype(F32).astype(BF16)
    radius = (first + lax.broadcasted_iota(jnp.int32, (8, 256), 0)).astype(F32) * (1.0 / RANGE)
    for level in range(4):

        def prepare(q, carry, level=level):
            half = core if level == 0 else (q // (1 << (level - 1))) % 2
            start = (half * 128).astype(F32)
            for side in range(2):
                index = (level * 8 + q) * 2 + side
                rows = par[level, q, side * 8 : side * 8 + 8, :]
                place = rows[4:5] - start
                weight = rows[0:4]
                high = weight.astype(BF16)
                rest = (weight - high.astype(F32)).astype(BF16)
                tops = jnp.zeros((128, 256), BF16)
                tails = jnp.zeros((128, 256), BF16)
                for tap in range(4):
                    hit = beam == (place + float(tap)).astype(BF16)
                    tops = jnp.where(hit, high[tap : tap + 1], tops)
                    tails = jnp.where(hit, rest[tap : tap + 1], tails)
                bank[index, 0:128] = tops
                bank[index, 128:256] = tails
                cosine, sine = turn_by(rows[6:7] + rows[7:8] * radius)
                wave[index, 0] = SCALE * cosine
                wave[index, 1] = SCALE * sine
                step = rows[7:8] * (8.0 / RANGE)
                step2 = step * step
                rates[index, 0:1] = 1.0 - 0.5 * step2 + step2 * step2 * (1.0 / 24.0)
                rates[index, 1:2] = step - step * step2 * (1.0 / 6.0)
                rates[index, 2:3] = jnp.abs(rows[5:6])
                rates[index, 3:4] = rows[5:6]
            return carry

        lax.fori_loop(0, 8, prepare, 0)

    maty_wait(0, 1)
    maty_relay(0).start()

    row8 = lax.broadcasted_iota(jnp.int32, (8, 128), 0)

    def run_level(level, sub):
        source, target = split.at[level % 2], split.at[(level + 1) % 2]
        start = first + sub * ROWS
        bins = start + jnp.where(low, ROWS + row8, row8 - 8)
        inside = jnp.where((bins >= 0) & (bins < RANGE), 1.0, 0.0).astype(F32)

        def multiply(q, part):
            index = (level * 8 + q) * 2
            for side in range(2):
                if level == 0:
                    slot = 2 * q + side
                else:
                    bit = 1 << (level - 1)
                    half = (q // bit) % 2
                    slot = (q - half * bit + side * bit) * 2 + half
                x = source[slot]
                w = bank[index + side]
                high, rest = w[0:128], w[128:256]
                part[side] = jnp.dot(
                    jnp.concatenate([x, x[:, 0:128]], axis=1),
                    jnp.concatenate([high, high, rest], axis=0),
                    preferred_element_type=F32,
                )

        def combine(q, part):
            index = (level * 8 + q) * 2
            for half in range(2):
                lanes = slice(half * 128, half * 128 + 128)

                def load(side, comp, t):
                    return part[side, t * 16 + comp * 8 : t * 16 + comp * 8 + 8, lanes]

                cosine = [wave[index + s, 0, :, lanes] for s in range(2)]
                sine = [wave[index + s, 1, :, lanes] for s in range(2)]
                step_c = [jnp.broadcast_to(rates[index + s, 0:1, lanes], (8, 128)) for s in range(2)]
                step_s = [jnp.broadcast_to(rates[index + s, 1:2, lanes], (8, 128)) for s in range(2)]
                amount = [jnp.broadcast_to(rates[index + s, 2:3, lanes], (8, 128)) for s in range(2)]
                ahead = [jnp.broadcast_to(rates[index + s, 3:4, lanes], (8, 128)) > 0.0 for s in range(2)]
                back_c = [cosine[s] * step_c[s] + sine[s] * step_s[s] for s in range(2)]
                back_s = [sine[s] * step_c[s] - cosine[s] * step_s[s] for s in range(2)]
                up, down = {}, {}
                for s in range(2):
                    for comp in range(2):
                        up[s, comp, 0] = pltpu.roll(load(s, comp, 0), 7, 0)
                        down[s, comp, -1] = pltpu.roll(load(s, comp, TILES - 1), 1, 0)
                previous = None
                for t in range(TILES if level < 3 else TILES - 1):
                    if t == TILES - 1:
                        if sub + 1 < SUBS:
                            for s in range(2):
                                wave[index + s, 0, :, lanes] = cosine[s]
                                wave[index + s, 1, :, lanes] = sine[s]
                        for s in range(2):
                            cosine[s] = jnp.where(low, cosine[s], back_c[s])
                            sine[s] = jnp.where(low, sine[s], back_s[s])
                    total = [None, None]
                    for s in range(2):
                        moved = []
                        for comp in range(2):
                            center = load(s, comp, t)
                            if t + 1 < TILES:
                                up[s, comp, t + 1] = pltpu.roll(load(s, comp, t + 1), 7, 0)
                                following = up[s, comp, t + 1]
                            else:
                                following = pltpu.roll(load(s, comp, 0), 7, 0)
                            down[s, comp, t] = pltpu.roll(center, 1, 0)
                            after = jnp.where(row8 == 7, following, up[s, comp, t])
                            before = jnp.where(row8 == 0, down[s, comp, t - 1], down[s, comp, t])
                            beside = jnp.where(ahead[s], after, before)
                            moved.append(center + amount[s] * (beside - center))
                        real = moved[0] * cosine[s] - moved[1] * sine[s]
                        imag = moved[0] * sine[s] + moved[1] * cosine[s]
                        total = [real, imag] if s == 0 else [total[0] + real, total[1] + imag]
                        if t < TILES - 1:
                            cosine[s], sine[s] = (
                                cosine[s] * step_c[s] - sine[s] * step_s[s],
                                sine[s] * step_c[s] + cosine[s] * step_s[s],
                            )
                    if level < 3:
                        if t == TILES - 1:
                            total = [v * inside for v in total]
                        both = jnp.concatenate(total, axis=0)
                        high = both.astype(BF16)
                        target[q * 2 + half, t * 16 : t * 16 + 16, 0:128] = high
                        target[q * 2 + half, t * 16 : t * 16 + 16, 128:256] = (both - high.astype(F32)).astype(BF16)
                    elif t % 2 == 0:
                        previous = total
                    else:
                        for comp in range(2):
                            row = comp * ROWS + (t // 2) * 16
                            gathered[0][sub][core * 8 + q, row : row + 16, lanes] = jnp.concatenate(
                                [previous[comp], total[comp]], axis=0
                            ).astype(BF16)
                if level == 3 and sub + 1 < SUBS:
                    for s in range(2):
                        wave[index + s, 0, :, lanes] = cosine[s]
                        wave[index + s, 1, :, lanes] = sine[s]

        def two(pair, carry):
            multiply(2 * pair + 1, part1)
            combine(2 * pair, part0)
            multiply((2 * pair + 2) % 8, part0)
            combine(2 * pair + 1, part1)
            return carry

        multiply(0, part0)
        lax.fori_loop(0, 4, two, 0)

    own_half = pl.ds(core * 8, 8)
    pending = []

    def start(copy):
        copy.start()
        pending.append(copy)

    def core_copy(place, sub):
        ref = gathered[place][sub].at[own_half]
        n = place * 2 + sub
        return remote(ref, ref, core_send.at[n], core_recv.at[n], sibling)

    def core_wait(place, sub):
        if place == 3:
            for way in range(2):
                core_far(way, sub, 1 - core).wait_recv()
            return
        ref = gathered[place][sub].at[pl.ds((1 - core) * 8, 8)]
        n = place * 2 + sub
        remote(ref, ref, core_send.at[n], core_recv.at[n], sibling).wait_recv()

    def core_far(way, sub, side=core):
        ref = gathered[3][sub].at[pl.ds(side * 8 + way * 4, 4)]
        n = 6 + sub if way == 0 else 8 + sub
        return remote(ref, ref, core_send.at[n], core_recv.at[n], sibling)

    def ring_copy(way, sub):
        n = way * 2 + sub
        return remote(
            gathered[0][sub].at[own_half], gathered[1 + way][sub].at[own_half],
            ring_send.at[n], ring_recv.at[n], (z_next, z_prev)[way],
        )

    def relay_copy(way, sub):
        n = way * 2 + sub
        quarter = pl.ds(core * 8 + way * 4, 4)
        return remote(
            gathered[1 + way][sub].at[quarter], gathered[3][sub].at[quarter],
            relay_send.at[n], relay_recv.at[n], (z_next, z_prev)[way],
        )

    for sub in range(SUBS):

        def wait_child(step, carry, sub=sub):
            child_copy(sub, step, (a + step) % 16).wait_recv()
            return carry

        lax.fori_loop(1, 16, wait_child, 0)
        keep_copy(sub).wait()

        def halve(n, carry, sub=sub):
            power = received[sub, n, TILES * 16 : TILES * 16 + 16].astype(F32)[0:1]
            x = received[sub, n, 0 : TILES * 16].astype(F32) * jnp.exp2(power)
            high = x.astype(BF16)
            split[0, n, :, 0:128] = high
            split[0, n, :, 128:256] = (x - high.astype(F32)).astype(BF16)
            return carry

        lax.fori_loop(0, 16, halve, 0)
        for level in range(4):
            run_level(level, sub)
        for way in range(2):
            start(ring_copy(way, sub))
        start(core_copy(0, sub))
        if sub == 0:
            maty_wait(1, 3)
            maty_relay(1).start()

    def relay(sub):
        for way in range(2):
            ring_copy(way, sub).wait_recv()
            start(relay_copy(way, sub))
            start(core_copy(1 + way, sub))

    def far(sub):
        for way in range(2):
            relay_copy(way, sub).wait_recv()
            start(core_far(way, sub))

    def tile_copy(n):
        return remote(sent_tiles.at[n], got_tiles.at[n], tile_send.at[n], tile_recv.at[n], x_pair)

    lane = lax.broadcasted_iota(jnp.int32, (512, 128), 1)

    def place_tile(early, late, side, place):
        where = (side * 4 + (z + (0, 3, 1, 2)[place]) % 4) * 128
        lanes = pl.ds(pl.multiple_of(where, 128), 128)
        out[0, :, lanes] = jnp.where(lane < 64, early, pltpu.roll(late, 64, 1))
        out[1, :, lanes] = jnp.where(lane < 64, pltpu.roll(early, 64, 1), late)

    def product(place, sub, tile):
        n = place * 2 + sub
        for k in range(8):
            block = info_s[0, k] if tile else sources[0, k]
            columns[:, k * 256 : k * 256 + 256] = gathered[place][sub][(block % 2) * 8 + block // 2]
        result = lax.dot_general(
            wide[tile], columns[...], (((1,), (1,)), ((), ())), preferred_element_type=F32
        )
        if tile:
            sent_tiles[n] = result.astype(BF16)
            start(tile_copy(n))
        elif sub == 0:
            held[place] = result
        else:
            place_tile(held[place], result, xh, place)

    for sub in range(SUBS):
        core_wait(0, sub)
        product(0, sub, 0)
    relay(0)
    info_copy.wait()
    listed = pltpu.make_async_copy(info_got, info_s, local_sem.at[2])
    listed.start()
    listed.wait()
    for piece, step in ((0, 3), (0, 2), (1, 1), (1, 2)):
        maty_wait(piece, step)
    other_live = info_s[1, 0]
    for k in range(8):
        wide[1, :, k * 256 : k * 256 + 256] = other_mat[k] * jnp.where(k < other_live, 1.0, 0.0).astype(BF16)
    product(0, 0, 1)
    product(0, 1, 1)

    def both(place, sub):
        core_wait(place, sub)
        product(place, sub, 1)
        product(place, sub, 0)

    for place in (1, 2):
        core_wait(place, 0)
        product(place, 0, 1)
    relay(1)
    product(1, 0, 0)
    product(2, 0, 0)
    for place in (1, 2):
        core_wait(place, 1)
        product(place, 1, 1)
    far(0)
    core_wait(3, 0)
    product(3, 0, 1)
    product(1, 1, 0)
    product(2, 1, 0)
    product(3, 0, 0)
    far(1)
    both(3, 1)
    for place in range(4):
        for sub in range(SUBS):
            tile_copy(place * 2 + sub).wait_recv()
        place_tile(got_tiles[place * 2].astype(F32), got_tiles[place * 2 + 1].astype(F32), 1 - xh, place)

    for copy in pending:
        copy.wait_send()
    for step in (1, 2, 3):
        pary_copy(step).wait_send()
        for piece in range(2):
            (maty_relay(piece) if step == 2 else maty_copy(piece, step)).wait_send()
    for part in range(8):
        mat_first(p, part).wait_send()
        mat_second(there, part).wait_send()

    def wait_last_sent(step, carry):
        child_copy(1, step, a).wait_send()
        return carry

    lax.fori_loop(1, 16, wait_last_sent, 0)

    def wait_par_sent(step, carry):
        par_copy(step, me).wait_send()
        return carry

    lax.fori_loop(1, 8, wait_par_sent, 0)


def shards(child, taps, bands, shifts, bases, slopes, sources, counts, matrices):
    counts = counts.reshape(1, 1)
    matrices = matrices[0]
    vmem = pl.BlockSpec(memory_space=pltpu.VMEM)
    smem = pl.BlockSpec(memory_space=pltpu.SMEM)
    hbm = pl.BlockSpec(memory_space=pl.ANY)
    dma = pltpu.SemaphoreType.DMA
    scratch = [
        pltpu.VMEM((2, 256, 1024), F32),
        pltpu.VMEM((8, 512, 256), BF16),
        pltpu.VMEM((16, 2, TILES, 2, 8, 128), F32),
        pltpu.VMEM((2, 2, 2, 8, 128), F32),
        pltpu.VMEM((16, 2, TILES * 16 + 16, 128), jnp.int16),
        pltpu.VMEM((SUBS, 16, TILES * 16 + 16, 128), jnp.int16),
        pltpu.VMEM((2, 16, TILES * 16, 256), BF16),
        pltpu.VMEM((2, TILES * 16, 256), F32),
        pltpu.VMEM((2, TILES * 16, 256), F32),
        pltpu.VMEM((64, 256, 256), BF16),
        pltpu.VMEM((64, 2, 8, 256), F32),
        pltpu.VMEM((64, 8, 256), F32),
        pltpu.VMEM((4, 16, 256), F32),
        pltpu.VMEM((4, 8, 16, 256), F32),
        *[pltpu.VMEM((16, 128, 256), BF16) for _ in range(8)],
        pltpu.VMEM((8, 512, 256), BF16),
        pltpu.VMEM((2, 512, 2048), BF16),
        pltpu.VMEM((128, 2048), BF16),
        pltpu.VMEM((8, 512, 128), BF16),
        pltpu.VMEM((8, 512, 128), BF16),
        pltpu.VMEM((4, 512, 128), F32),
        pltpu.VMEM((8, 128), jnp.int32),
        pltpu.VMEM((8, 128), jnp.int32),
        pltpu.SMEM((8, 128), jnp.int32),
        dma((2, 16)), dma((2, 16)),
        dma((2,)), dma((2,)),
        dma((8,)), dma((8,)),
        dma((4,)), dma((4,)),
        dma((16,)), dma((16,)),
        dma((8,)), dma((8,)),
        dma((4,)), dma((4,)),
        dma((4,)), dma((4,)),
        dma((10,)), dma((10,)),
        dma((8,)), dma((8,)),
        dma((1,)), dma((1,)),
        dma((5,)),
    ]
    return pl.pallas_call(
        kernel,
        out_shape=pltpu.VMEM((2, 512, 1024), F32),
        in_specs=[hbm] + [vmem] * 7 + [hbm] + [smem] * 2,
        out_specs=vmem,
        scratch_shapes=scratch,
        compiler_params=pltpu.CompilerParams(
            collective_id=0, has_side_effects=True, vmem_limit_bytes=56 * 2**20
        ),
    )(child, taps, bands, shifts, bases, slopes, sources, counts, matrices, sources, counts)


def solution(mesh):
    placed = (
        P(None, "aperture", "range"),
        P(None, None, None, "aperture"),
        P(None, None, "aperture"),
        P(None, None, "aperture"),
        P(None, None, "aperture"),
        P(None, None, "aperture"),
        P("aperture", None),
        P("aperture"),
        P("aperture", None, None, None),
    )
    return jax.shard_map(
        shards, mesh=mesh, in_specs=placed, out_specs=P(None, "aperture", "range"), check_vma=False
    )
```

```python
import functools

import jax
import jax.numpy as jnp
import numpy as np
from jax import lax
from jax.experimental import pallas as pl
from jax.experimental.pallas import tpu as pltpu
from jax.sharding import PartitionSpec as P

RANGE = 8192
SCALE = 0.70710678
MESH = pl.DeviceIdType.MESH
SUBS = 2
ROWS = 64
TILES = 9
F32 = jnp.float32
BF16 = jnp.bfloat16


def turn_by(angle):
    quarters = jnp.round(angle * (2.0 / np.pi))
    x = angle - quarters * 1.5703125
    x = x - quarters * 4.838267948966e-4
    x2 = x * x
    sine = x + x * x2 * (-1.6666654611e-1 + x2 * (8.3321608736e-3 - x2 * 1.9515295891e-4))
    cosine = 1.0 - 0.5 * x2 + x2 * x2 * (4.166664568298827e-2 + x2 * (-1.388731625493765e-3 + x2 * 2.443315711809948e-5))
    part = quarters - 4.0 * jnp.floor(quarters * 0.25)
    odd = (part == 1.0) | (part == 3.0)
    first = jnp.where(odd, sine, cosine)
    second = jnp.where(odd, cosine, sine)
    first = jnp.where((part == 1.0) | (part == 2.0), -first, first)
    second = jnp.where(part >= 2.0, -second, second)
    return first, second


def kernel(
    child_h, taps, bands, shifts, bases, slopes, sources_v, counts_v, matrices, sources, counts,
    out,
    child, own_mat, staged, edges, coded, received, split, part0, part1, bank, wave, rates, own_par, par,
    g00, g01, g10, g11, g20, g21, g30, g31,
    other_mat, wide, columns, sent_tiles, got_tiles, held, info, info_got, info_s,
    a2a_send, a2a_recv, edge_send, edge_recv, par_send, par_recv, pary_send, pary_recv,
    mat_send, mat_recv, maty_send, maty_recv, ring_send, ring_recv, relay_send, relay_recv,
    core_send, core_recv, tile_send, tile_recv, info_send, info_recv, local_sem,
):
    gathered = ((g00, g01), (g10, g11), (g20, g21), (g30, g31))
    a = lax.axis_index("aperture")
    p = lax.axis_index("range")
    core, z, xh = a % 2, (a // 2) % 4, a // 8
    y, xl = p // 2, p % 2
    me = a // 2
    sibling = (me * 2 + 1 - core, p)
    z_next = (xh * 8 + ((z + 1) % 4) * 2 + core, p)
    z_prev = (xh * 8 + ((z + 3) % 4) * 2 + core, p)
    x_pair = ((a + 8) % 16, p)
    x_side = ((a + 8) % 16, y * 2 + 1 - xl)
    r_next = (a, (p + 1) % 8)
    r_prev = (a, (p + 7) % 8)

    def y_peer(step):
        return (a, ((y + step) % 4) * 2 + xl)

    load_child = pltpu.make_async_copy(child_h, child, local_sem.at[3])
    load_child.start()
    load_mat = pltpu.make_async_copy(matrices, own_mat, local_sem.at[4])
    load_mat.start()

    barrier = pltpu.get_barrier_semaphore()

    def greet(step, carry):
        pl.semaphore_signal(barrier, inc=1, device_id=((a + step) % 16, p), device_id_type=MESH)
        return carry

    lax.fori_loop(1, 16, greet, 0)
    for peer in (x_side, r_next, r_prev, y_peer(1), y_peer(2), y_peer(3)):
        pl.semaphore_signal(barrier, inc=1, device_id=peer, device_id_type=MESH)

    for level in range(4):
        for side in range(2):
            row = side * 8
            own_par[level, row : row + 4, :] = taps[level, side]
            own_par[level, row + 4 : row + 5, :] = bands[level, side : side + 1, :].astype(F32)
            own_par[level, row + 5 : row + 6, :] = shifts[level, side : side + 1, :]
            own_par[level, row + 6 : row + 7, :] = bases[level, side : side + 1, :]
            own_par[level, row + 7 : row + 8, :] = slopes[level, side : side + 1, :]
    info[...] = jnp.zeros((8, 128), jnp.int32)
    info[0:1, 0:8] = sources_v[...]
    info[1:2, 0:1] = counts_v[...]

    load_child.wait()

    def turn(k, carry):
        for comp in range(2):
            for half in range(2):
                block = child[comp, half * 128 : half * 128 + 128, pl.ds(pl.multiple_of(k * 128, 128), 128)]
                block = block.T.reshape(2, 8, 8, 128)
                for sub in range(2):
                    staged[k * 2 + sub, half, 0:8, comp] = block[sub]
        return carry

    lax.fori_loop(0, 8, turn, 0)

    pl.semaphore_wait(barrier, 21)

    def remote(src, dst, send, recv, to):
        return pltpu.make_async_remote_copy(
            src_ref=src, dst_ref=dst, send_sem=send, recv_sem=recv, device_id=to, device_id_type=MESH
        )

    there = p + 1 - 2 * (p % 2)

    def mat_first(n, part):
        where = other_mat.at[pl.ds(n, 1), part * 64 : part * 64 + 64]
        return remote(
            matrices.at[pl.ds(n, 1), part * 64 : part * 64 + 64], where, mat_send.at[part], mat_recv.at[part], x_side
        )

    def mat_second(n, part):
        where = other_mat.at[pl.ds(n, 1), part * 64 : part * 64 + 64]
        return remote(where, where, mat_send.at[8 + part], mat_recv.at[8 + part], (a, there))

    def par_copy(step, slot):
        return remote(
            own_par.at[y], par.at[y, slot], par_send.at[step], par_recv.at[slot], ((a + 2 * step) % 16, p)
        )

    def send_par(step, carry):
        par_copy(step, me).start()
        return carry

    lax.fori_loop(1, 8, send_par, 0)
    info_copy = remote(info, info_got, info_send.at[0], info_recv.at[0], x_pair)
    info_copy.start()
    for part in range(8):
        mat_first(p, part).start()

    edge_next = remote(staged.at[15, :, 7], edges.at[0], edge_send.at[0], edge_recv.at[0], r_next)
    edge_prev = remote(staged.at[0, :, 0], edges.at[1], edge_send.at[1], edge_recv.at[1], r_prev)
    edge_next.start()
    edge_prev.start()
    low = lax.broadcasted_iota(jnp.int32, (8, 128), 0) < 4

    def fill(j, carry):
        for half in range(2):
            for comp in range(2):
                staged[j, half, 8, comp] = jnp.where(low, staged[j + 1, half, 0, comp], staged[j - 1, half, 7, comp])
        return carry

    def code(j, carry):
        for half in range(2):
            x = staged[j, half].reshape(TILES * 16, 128)
            most = jnp.max(jnp.abs(x), axis=0, keepdims=True)
            power = jnp.ceil(jnp.log2(jnp.maximum(most, 1e-30)) - 14.9999)
            coded[j, half, 0 : TILES * 16] = jnp.round(x * jnp.exp2(-power)).astype(jnp.int16)
            coded[j, half, TILES * 16 : TILES * 16 + 16] = jnp.broadcast_to(power, (16, 128)).astype(jnp.int16)
        return carry

    def fill_code(j, carry):
        return code(j, fill(j, carry))

    def child_copy(sub, step, slot):
        to = (a + step) % 16
        return remote(
            coded.at[(to // 2) * 2 + sub, to % 2],
            received.at[sub, slot],
            a2a_send.at[sub, step],
            a2a_recv.at[sub, slot],
            (to, p),
        )

    def keep_copy(sub):
        return pltpu.make_async_copy(coded.at[me * 2 + sub, core], received.at[sub, a], local_sem.at[sub])

    def send_children(sub, edge):
        last = 7 * sub

        def send_child(step, carry):
            @pl.when((((a + step) % 16) // 2 == last) == edge)
            def _():
                child_copy(sub, step, a).start()

            return carry

        lax.fori_loop(1, 16, send_child, 0)

        @pl.when((me == last) == edge)
        def _():
            keep_copy(sub).start()

    lax.fori_loop(1, 15, fill_code, 0)
    send_children(0, False)
    edge_next.wait()
    edge_prev.wait()
    has_prev = jnp.where(p > 0, 1.0, 0.0).astype(F32)
    has_next = jnp.where(p < 7, 1.0, 0.0).astype(F32)
    for half in range(2):
        for comp in range(2):
            staged[0, half, 8, comp] = jnp.where(low, staged[1, half, 0, comp], edges[0, half, comp] * has_prev)
            staged[15, half, 8, comp] = jnp.where(low, edges[1, half, comp] * has_next, staged[14, half, 7, comp])
    code(0, 0)
    code(15, 0)
    send_children(0, True)

    par[y, me] = own_par[y]

    def wait_par(step, carry):
        par_copy(step, (me + step) % 8).wait_recv()
        return carry

    lax.fori_loop(1, 8, wait_par, 0)

    def pary_copy(step):
        return remote(par.at[y], par.at[y], pary_send.at[step], pary_recv.at[step], y_peer(step))

    def pary_wait(step):
        there = (y + 4 - step) % 4
        remote(par.at[there], par.at[there], pary_send.at[step], pary_recv.at[step], y_peer(step)).wait_recv()

    for step in (1, 2, 3):
        pary_copy(step).start()

    def maty_copy(piece, step):
        own = pl.ds((there, p)[piece], 1)
        n = piece * 4 + step
        return remote(other_mat.at[own], other_mat.at[own], maty_send.at[n], maty_recv.at[n], y_peer(step))

    def far_piece(piece, step):
        p_far = ((y + 4 - step) % 4) * 2 + xl
        return pl.ds((p_far + 1 - 2 * (p_far % 2), p_far)[piece], 1)

    def maty_wait(piece, step):
        far = far_piece(piece, step)
        n = piece * 4 + step
        remote(other_mat.at[far], other_mat.at[far], maty_send.at[n], maty_recv.at[n], y_peer(step)).wait_recv()

    def maty_relay(piece):
        step = (1, 3)[piece]
        far = far_piece(piece, step)
        n = piece * 4 + 2
        return remote(other_mat.at[far], other_mat.at[far], maty_send.at[n], maty_recv.at[n], y_peer(step))

    for part in range(8):
        mat_first(there, part).wait_recv()
        mat_second(there, part).start()
    for step in (1, 3):
        maty_copy(0, step).start()

    def wait_sent(step, carry):
        child_copy(0, step, a).wait_send()
        return carry

    lax.fori_loop(1, 16, wait_sent, 0)
    send_children(1, False)
    send_children(1, True)
    for step in (1, 2, 3):
        pary_wait(step)
    for part in range(8):
        mat_second(p, part).wait_recv()
    for step in (3, 1):
        maty_copy(1, step).start()

    first = p * 1024 + me * (SUBS * ROWS)
    beam = lax.broadcasted_iota(jnp.int32, (128, 256), 0).astype(F32).astype(BF16)
    radius = (first + lax.broadcasted_iota(jnp.int32, (8, 256), 0)).astype(F32) * (1.0 / RANGE)
    for level in range(4):

        def prepare(q, carry, level=level):
            half = core if level == 0 else (q // (1 << (level - 1))) % 2
            start = (half * 128).astype(F32)
            for side in range(2):
                index = (level * 8 + q) * 2 + side
                rows = par[level, q, side * 8 : side * 8 + 8, :]
                place = rows[4:5] - start
                weight = rows[0:4]
                high = weight.astype(BF16)
                rest = (weight - high.astype(F32)).astype(BF16)
                tops = jnp.zeros((128, 256), BF16)
                tails = jnp.zeros((128, 256), BF16)
                for tap in range(4):
                    hit = beam == (place + float(tap)).astype(BF16)
                    tops = jnp.where(hit, high[tap : tap + 1], tops)
                    tails = jnp.where(hit, rest[tap : tap + 1], tails)
                bank[index, 0:128] = tops
                bank[index, 128:256] = tails
                cosine, sine = turn_by(rows[6:7] + rows[7:8] * radius)
                wave[index, 0] = SCALE * cosine
                wave[index, 1] = SCALE * sine
                step = rows[7:8] * (8.0 / RANGE)
                step2 = step * step
                rates[index, 0:1] = 1.0 - 0.5 * step2 + step2 * step2 * (1.0 / 24.0)
                rates[index, 1:2] = step - step * step2 * (1.0 / 6.0)
                rates[index, 2:3] = jnp.abs(rows[5:6])
                rates[index, 3:4] = rows[5:6]
            return carry

        lax.fori_loop(0, 8, prepare, 0)

    maty_wait(0, 1)
    maty_relay(0).start()

    row8 = lax.broadcasted_iota(jnp.int32, (8, 128), 0)

    def run_level(level, sub):
        source, target = split.at[level % 2], split.at[(level + 1) % 2]
        start = first + sub * ROWS
        bins = start + jnp.where(low, ROWS + row8, row8 - 8)
        inside = jnp.where((bins >= 0) & (bins < RANGE), 1.0, 0.0).astype(F32)

        def multiply(q, part):
            index = (level * 8 + q) * 2
            for side in range(2):
                if level == 0:
                    slot = 2 * q + side
                else:
                    bit = 1 << (level - 1)
                    half = (q // bit) % 2
                    slot = (q - half * bit + side * bit) * 2 + half
                x = source[slot]
                w = bank[index + side]
                high, rest = w[0:128], w[128:256]
                part[side] = jnp.dot(
                    jnp.concatenate([x, x[:, 0:128]], axis=1),
                    jnp.concatenate([high, high, rest], axis=0),
                    preferred_element_type=F32,
                )

        def combine(q, part):
            index = (level * 8 + q) * 2
            for half in range(2):
                lanes = slice(half * 128, half * 128 + 128)

                def load(side, comp, t):
                    return part[side, t * 16 + comp * 8 : t * 16 + comp * 8 + 8, lanes]

                cosine = [wave[index + s, 0, :, lanes] for s in range(2)]
                sine = [wave[index + s, 1, :, lanes] for s in range(2)]
                step_c = [jnp.broadcast_to(rates[index + s, 0:1, lanes], (8, 128)) for s in range(2)]
                step_s = [jnp.broadcast_to(rates[index + s, 1:2, lanes], (8, 128)) for s in range(2)]
                amount = [jnp.broadcast_to(rates[index + s, 2:3, lanes], (8, 128)) for s in range(2)]
                ahead = [jnp.broadcast_to(rates[index + s, 3:4, lanes], (8, 128)) > 0.0 for s in range(2)]
                back_c = [cosine[s] * step_c[s] + sine[s] * step_s[s] for s in range(2)]
                back_s = [sine[s] * step_c[s] - cosine[s] * step_s[s] for s in range(2)]
                up, down = {}, {}
                for s in range(2):
                    for comp in range(2):
                        up[s, comp, 0] = pltpu.roll(load(s, comp, 0), 7, 0)
                        down[s, comp, -1] = pltpu.roll(load(s, comp, TILES - 1), 1, 0)
                previous = None
                for t in range(TILES if level < 3 else TILES - 1):
                    if t == TILES - 1:
                        if sub + 1 < SUBS:
                            for s in range(2):
                                wave[index + s, 0, :, lanes] = cosine[s]
                                wave[index + s, 1, :, lanes] = sine[s]
                        for s in range(2):
                            cosine[s] = jnp.where(low, cosine[s], back_c[s])
                            sine[s] = jnp.where(low, sine[s], back_s[s])
                    total = [None, None]
                    for s in range(2):
                        moved = []
                        for comp in range(2):
                            center = load(s, comp, t)
                            if t + 1 < TILES:
                                up[s, comp, t + 1] = pltpu.roll(load(s, comp, t + 1), 7, 0)
                                following = up[s, comp, t + 1]
                            else:
                                following = pltpu.roll(load(s, comp, 0), 7, 0)
                            down[s, comp, t] = pltpu.roll(center, 1, 0)
                            after = jnp.where(row8 == 7, following, up[s, comp, t])
                            before = jnp.where(row8 == 0, down[s, comp, t - 1], down[s, comp, t])
                            beside = jnp.where(ahead[s], after, before)
                            moved.append(center + amount[s] * (beside - center))
                        real = moved[0] * cosine[s] - moved[1] * sine[s]
                        imag = moved[0] * sine[s] + moved[1] * cosine[s]
                        total = [real, imag] if s == 0 else [total[0] + real, total[1] + imag]
                        if t < TILES - 1:
                            cosine[s], sine[s] = (
                                cosine[s] * step_c[s] - sine[s] * step_s[s],
                                sine[s] * step_c[s] + cosine[s] * step_s[s],
                            )
                    if level < 3:
                        if t == TILES - 1:
                            total = [v * inside for v in total]
                        both = jnp.concatenate(total, axis=0)
                        high = both.astype(BF16)
                        target[q * 2 + half, t * 16 : t * 16 + 16, 0:128] = high
                        target[q * 2 + half, t * 16 : t * 16 + 16, 128:256] = (both - high.astype(F32)).astype(BF16)
                    elif t % 2 == 0:
                        previous = total
                    else:
                        for comp in range(2):
                            row = comp * ROWS + (t // 2) * 16
                            gathered[0][sub][core * 8 + q, row : row + 16, lanes] = jnp.concatenate(
                                [previous[comp], total[comp]], axis=0
                            ).astype(BF16)
                if level == 3 and sub + 1 < SUBS:
                    for s in range(2):
                        wave[index + s, 0, :, lanes] = cosine[s]
                        wave[index + s, 1, :, lanes] = sine[s]

        def two(pair, carry):
            multiply(2 * pair + 1, part1)
            combine(2 * pair, part0)
            multiply((2 * pair + 2) % 8, part0)
            combine(2 * pair + 1, part1)
            return carry

        multiply(0, part0)
        lax.fori_loop(0, 4, two, 0)

    own_half = pl.ds(core * 8, 8)
    pending = []

    def start(copy):
        copy.start()
        pending.append(copy)

    def core_copy(place, sub):
        ref = gathered[place][sub].at[own_half]
        n = place * 2 + sub
        return remote(ref, ref, core_send.at[n], core_recv.at[n], sibling)

    def core_wait(place, sub):
        if place == 3:
            for way in range(2):
                core_far(way, sub, 1 - core).wait_recv()
            return
        ref = gathered[place][sub].at[pl.ds((1 - core) * 8, 8)]
        n = place * 2 + sub
        remote(ref, ref, core_send.at[n], core_recv.at[n], sibling).wait_recv()

    def core_far(way, sub, side=core):
        ref = gathered[3][sub].at[pl.ds(side * 8 + way * 4, 4)]
        n = 6 + sub if way == 0 else 8 + sub
        return remote(ref, ref, core_send.at[n], core_recv.at[n], sibling)

    def ring_copy(way, sub, part):
        n = way * 2 + sub
        piece = pl.ds(core * 8 + part * 4, 4)
        return remote(
            gathered[0][sub].at[piece], gathered[1 + way][sub].at[piece],
            ring_send.at[n, part], ring_recv.at[n, part], (z_next, z_prev)[way],
        )

    def relay_copy(way, sub):
        n = way * 2 + sub
        quarter = pl.ds(core * 8 + way * 4, 4)
        return remote(
            gathered[1 + way][sub].at[quarter], gathered[3][sub].at[quarter],
            relay_send.at[n], relay_recv.at[n], (z_next, z_prev)[way],
        )

    for sub in range(SUBS):

        def wait_child(step, carry, sub=sub):
            child_copy(sub, step, (a + step) % 16).wait_recv()
            return carry

        lax.fori_loop(1, 16, wait_child, 0)
        keep_copy(sub).wait()

        def halve(n, carry, sub=sub):
            power = received[sub, n, TILES * 16 : TILES * 16 + 16].astype(F32)[0:1]
            x = received[sub, n, 0 : TILES * 16].astype(F32) * jnp.exp2(power)
            high = x.astype(BF16)
            split[0, n, :, 0:128] = high
            split[0, n, :, 128:256] = (x - high.astype(F32)).astype(BF16)
            return carry

        lax.fori_loop(0, 16, halve, 0)
        for level in range(4):
            run_level(level, sub)
            if sub == 0 and level == 1:
                maty_wait(1, 3)
                maty_relay(1).start()
        for way in range(2):
            for part in (way, 1 - way):
                start(ring_copy(way, sub, part))
        start(core_copy(0, sub))

    def relay(sub):
        for way in range(2):
            ring_copy(way, sub, way).wait_recv()
            start(relay_copy(way, sub))
        for way in range(2):
            ring_copy(way, sub, 1 - way).wait_recv()
            start(core_copy(1 + way, sub))

    def far(sub):
        for way in range(2):
            relay_copy(way, sub).wait_recv()
            start(core_far(way, sub))

    def tile_copy(n):
        return remote(sent_tiles.at[n], got_tiles.at[n], tile_send.at[n], tile_recv.at[n], x_pair)

    lane = lax.broadcasted_iota(jnp.int32, (512, 128), 1)

    def place_tile(early, late, side, place):
        where = (side * 4 + (z + (0, 3, 1, 2)[place]) % 4) * 128
        lanes = pl.ds(pl.multiple_of(where, 128), 128)
        out[0, :, lanes] = jnp.where(lane < 64, early, pltpu.roll(late, 64, 1))
        out[1, :, lanes] = jnp.where(lane < 64, pltpu.roll(early, 64, 1), late)

    def product(place, sub, tile):
        n = place * 2 + sub
        for k in range(8):
            block = info_s[0, k] if tile else sources[0, k]
            columns[:, k * 256 : k * 256 + 256] = gathered[place][sub][(block % 2) * 8 + block // 2]
        result = lax.dot_general(
            wide[tile], columns[...], (((1,), (1,)), ((), ())), preferred_element_type=F32
        )
        if tile:
            sent_tiles[n] = result.astype(BF16)
            start(tile_copy(n))
        elif sub == 0:
            held[place] = result
        else:
            place_tile(held[place], result, xh, place)

    load_mat.wait()
    live = counts[0, 0]
    for k in range(8):
        wide[0, :, k * 256 : k * 256 + 256] = own_mat[k] * jnp.where(k < live, 1.0, 0.0).astype(BF16)

    for sub in range(SUBS):
        core_wait(0, sub)
        product(0, sub, 0)
    info_copy.wait()
    listed = pltpu.make_async_copy(info_got, info_s, local_sem.at[2])
    listed.start()
    listed.wait()
    other_live = info_s[1, 0]

    def widen(piece, step):
        p_far = ((y + 4 - step) % 4) * 2 + xl
        k = (p_far + 1 - 2 * (p_far % 2), p_far)[piece]
        where = pl.ds(pl.multiple_of(k * 256, 256), 256)
        wide[1, :, where] = other_mat[k] * jnp.where(k < other_live, 1.0, 0.0).astype(BF16)

    for piece, step in ((0, 0), (1, 0), (0, 1), (1, 3)):
        widen(piece, step)
    relay(0)
    for piece, step in ((0, 3), (0, 2), (1, 1), (1, 2)):
        maty_wait(piece, step)
        widen(piece, step)
    product(0, 0, 1)
    product(0, 1, 1)

    def both(place, sub):
        core_wait(place, sub)
        product(place, sub, 1)
        product(place, sub, 0)

    for place in (1, 2):
        core_wait(place, 0)
        product(place, 0, 1)
    relay(1)
    product(1, 0, 0)
    product(2, 0, 0)
    for place in (1, 2):
        core_wait(place, 1)
        product(place, 1, 1)
    far(0)
    core_wait(3, 0)
    product(3, 0, 1)
    product(1, 1, 0)
    product(2, 1, 0)
    product(3, 0, 0)
    far(1)
    both(3, 1)
    for place in range(4):
        for sub in range(SUBS):
            tile_copy(place * 2 + sub).wait_recv()
        place_tile(got_tiles[place * 2].astype(F32), got_tiles[place * 2 + 1].astype(F32), 1 - xh, place)

    for copy in pending:
        copy.wait_send()
    for step in (1, 2, 3):
        pary_copy(step).wait_send()
        for piece in range(2):
            (maty_relay(piece) if step == 2 else maty_copy(piece, step)).wait_send()
    for part in range(8):
        mat_first(p, part).wait_send()
        mat_second(there, part).wait_send()

    def wait_last_sent(step, carry):
        child_copy(1, step, a).wait_send()
        return carry

    lax.fori_loop(1, 16, wait_last_sent, 0)

    def wait_par_sent(step, carry):
        par_copy(step, me).wait_send()
        return carry

    lax.fori_loop(1, 8, wait_par_sent, 0)


def shards(child, taps, bands, shifts, bases, slopes, sources, counts, matrices):
    counts = counts.reshape(1, 1)
    matrices = matrices[0]
    vmem = pl.BlockSpec(memory_space=pltpu.VMEM)
    smem = pl.BlockSpec(memory_space=pltpu.SMEM)
    hbm = pl.BlockSpec(memory_space=pl.ANY)
    dma = pltpu.SemaphoreType.DMA
    scratch = [
        pltpu.VMEM((2, 256, 1024), F32),
        pltpu.VMEM((8, 512, 256), BF16),
        pltpu.VMEM((16, 2, TILES, 2, 8, 128), F32),
        pltpu.VMEM((2, 2, 2, 8, 128), F32),
        pltpu.VMEM((16, 2, TILES * 16 + 16, 128), jnp.int16),
        pltpu.VMEM((SUBS, 16, TILES * 16 + 16, 128), jnp.int16),
        pltpu.VMEM((2, 16, TILES * 16, 256), BF16),
        pltpu.VMEM((2, TILES * 16, 256), F32),
        pltpu.VMEM((2, TILES * 16, 256), F32),
        pltpu.VMEM((64, 256, 256), BF16),
        pltpu.VMEM((64, 2, 8, 256), F32),
        pltpu.VMEM((64, 8, 256), F32),
        pltpu.VMEM((4, 16, 256), F32),
        pltpu.VMEM((4, 8, 16, 256), F32),
        *[pltpu.VMEM((16, 128, 256), BF16) for _ in range(8)],
        pltpu.VMEM((8, 512, 256), BF16),
        pltpu.VMEM((2, 512, 2048), BF16),
        pltpu.VMEM((128, 2048), BF16),
        pltpu.VMEM((8, 512, 128), BF16),
        pltpu.VMEM((8, 512, 128), BF16),
        pltpu.VMEM((4, 512, 128), F32),
        pltpu.VMEM((8, 128), jnp.int32),
        pltpu.VMEM((8, 128), jnp.int32),
        pltpu.SMEM((8, 128), jnp.int32),
        dma((2, 16)), dma((2, 16)),
        dma((2,)), dma((2,)),
        dma((8,)), dma((8,)),
        dma((4,)), dma((4,)),
        dma((16,)), dma((16,)),
        dma((8,)), dma((8,)),
        dma((4, 2)), dma((4, 2)),
        dma((4,)), dma((4,)),
        dma((10,)), dma((10,)),
        dma((8,)), dma((8,)),
        dma((1,)), dma((1,)),
        dma((5,)),
    ]
    return pl.pallas_call(
        kernel,
        out_shape=pltpu.VMEM((2, 512, 1024), F32),
        in_specs=[hbm] + [vmem] * 7 + [hbm] + [smem] * 2,
        out_specs=vmem,
        scratch_shapes=scratch,
        compiler_params=pltpu.CompilerParams(
            collective_id=0, has_side_effects=True, vmem_limit_bytes=56 * 2**20
        ),
    )(child, taps, bands, shifts, bases, slopes, sources, counts, matrices, sources, counts)


def solution(mesh):
    placed = (
        P(None, "aperture", "range"),
        P(None, None, None, "aperture"),
        P(None, None, "aperture"),
        P(None, None, "aperture"),
        P(None, None, "aperture"),
        P(None, None, "aperture"),
        P("aperture", None),
        P("aperture"),
        P("aperture", None, None, None),
    )
    return jax.shard_map(
        shards, mesh=mesh, in_specs=placed, out_specs=P(None, "aperture", "range"), check_vma=False
    )
```
